512 devices in a mesh: dir: 8 (over y_lo, x), space: 64 (over z, y_hi, core).
Axes of the slice: x: 4, y: 4 (y_hi: 2, y_lo: 2; y = y_hi * 2 + y_lo), z: 16, core: 2. Of those that a mesh axis runs over, the one named last changes fastest.
Arguments:
- logk: float32 [4, 256, 1024], P(None, 'space'), may hold values from -3 to 3
- storage: float32 [4, 256, 1024], P(None, 'space'), may hold values from 0.5 to 4
- head0: float32 [4, 256, 1024], P(None, 'space'), may hold values from -4 to 4
- support: int32 [4, 256, 1024], P(None, 'space'), may hold values from 0 to 2047
- kweight: float32 [4, 256, 1024], P(None, 'space'), may hold values from 0.1 to 1
- fixed: int32 [256, 1024], P('space'), may hold values 0 or 1
- directions: float32 [32, 2048], P('dir'), may hold values from -4 to 4
- wells: int32 [1024], replicated, may hold values from 0 to 1048575
- rates: float32 [1024], replicated, may hold values from -8 to 8
Outputs:
- head: float32 [4, 256, 1024], P(None, 'space')
- sensitivity: float32 [32, 4, 256, 1024], P('dir', None, 'space')
The draws below stay inside these ranges and needn't reach their ends.
All inputs are finite; a program needn't handle non-finite values. No bound on the sum of `fixed` on one device may be relied on, other than what follows from the above.
Results may differ from the reference program's by a relative error of at most 0.00002.
Values sent between devices are 32-bit elements; how exact they have to be, the bound alone decides.
No kernel may reach another device: no remote copies, remote signals or barrier semaphores. Data moves between devices by JAX's collectives and lax.ppermute only.
A program may use at most 64 MiB of HBM per device.

```python
import math
import jax
import jax.numpy as jnp
from jax import lax

NY = 1024
L = 4
STEPS = 2
SWEEPS = 2
PILOTS = 2048
S = 4
NX = 256
DIRS = 32
WELLS = 1024


def set_ends(values, key, low, largest):
    longest = values.shape.index(max(values.shape))
    spots = []
    for shift in (0, 1):
        where = [jax.random.randint(jax.random.fold_in(key, axis), (), 0, length) for axis, length in enumerate(values.shape)]
        where[longest] = (where[longest] + shift) % values.shape[longest]
        spots.append(tuple(where))
    return values.at[spots[0]].set(low).at[spots[1]].set(largest)


def block_scale(rng, dims, pieces, least, top_value):
    level, own = 1.0, jax.random.fold_in(rng, 6)
    for position, blocks in pieces:
        heights = jnp.exp(jax.random.uniform(jax.random.fold_in(own, position), (blocks,), jnp.float32, least / len(pieces), top_value / len(pieces)))
        level = level * jnp.repeat(heights, dims[position] // blocks).reshape([-1 if axis == position else 1 for axis in range(len(dims))])
    return level


def centred(key, dims, width, bound, pieces=(), dtype=jnp.bfloat16):
    level = block_scale(key, dims, pieces, -0.22, 0.18) if pieces else 1.0
    values = jax.random.normal(key, dims, jnp.float32) * width * level
    return jnp.minimum(jnp.maximum(values, -bound), bound).astype(dtype)


def setup_inputs(seed: int = 0) -> dict:
    key_list = jax.random.split(jax.random.key(seed), 10)
    logk = centred(key_list[0], (L, NX, NY), 1.0, 3.0, ((1, 64),), jnp.float32)
    storage = jnp.clip(jnp.exp(math.log(4.0) - 2.0794415 * jax.random.uniform(key_list[1], (L, NX, NY), jnp.float32) ** block_scale(key_list[1], (L, NX, NY), ((1, 64),), -0.2, 0.2)), 0.5, 4.0)
    head0 = centred(key_list[2], (L, NX, NY), 1.0, 4.0, ((1, 64),), jnp.float32)
    support = set_ends(jax.random.randint(key_list[3], (S, NX, NY), 0, PILOTS), jax.random.fold_in(key_list[3], 1), 0, PILOTS - 1).astype(jnp.int32)
    kweight = jnp.clip(0.1 + 0.9 * jax.random.uniform(key_list[4], (S, NX, NY), jnp.float32) ** block_scale(key_list[4], (S, NX, NY), ((1, 64),), -0.2, 0.2), 0.1, 1.0)
    fixed = set_ends((jax.random.randint(key_list[5], (NX, NY), 0, 8) < 1).astype(jnp.int32), jax.random.fold_in(key_list[5], 1), 0, 1)
    directions = centred(key_list[6], (DIRS, PILOTS), 1.0, 4.0, ((0, 8),), jnp.float32)
    wells = set_ends(jax.random.randint(key_list[7], (WELLS,), 0, L * NX * NY), jax.random.fold_in(key_list[7], 1), 0, (L * NX * NY) - 1).astype(jnp.int32)
    rates = centred(key_list[8], (WELLS,), 2.0, 8.0, (), jnp.float32)
    return {"logk": logk, "storage": storage, "head0": head0, "support": support, "kweight": kweight, "fixed": fixed, "directions": directions, "wells": wells, "rates": rates}


vertical_ratio = 0.3


def face_values(logk):
    tx = jnp.pad(jnp.exp(0.5 * (logk[:, 1:] + logk[:, :-1])), ((0, 0), (1, 1), (0, 0)))
    ty = jnp.pad(jnp.exp(0.5 * (logk[:, :, 1:] + logk[:, :, :-1])), ((0, 0), (0, 0), (1, 1)))
    tz = vertical_ratio * jnp.pad(jnp.exp(0.5 * (logk[1:] + logk[:-1])), ((1, 1), (0, 0), (0, 0)))
    return tx, ty, tz


def neighbor_sum(tx, ty, tz, padded):
    center = padded[..., 1:-1, 1:-1]
    widths = [(0, 0)] * (center.ndim - 3) + [(1, 1), (0, 0), (0, 0)]
    vertical = jnp.pad(center, widths)
    total = tx[..., 1:, :] * padded[..., 2:, 1:-1] + tx[..., :-1, :] * padded[..., :-2, 1:-1]
    total = total + ty[..., 1:] * padded[..., 1:-1, 2:] + ty[..., :-1] * padded[..., 1:-1, :-2]
    total = total + tz[..., 1:, :, :] * vertical[..., 2:, :, :] + tz[..., :-1, :, :] * vertical[..., :-2, :, :]
    return total


def pad_plane(field):
    widths = [(0, 0)] * (field.ndim - 2) + [(1, 1), (1, 1)]
    return jnp.pad(field, widths)


def reference(logk, storage, head0, support, kweight, fixed, directions, wells, rates):
    tx, ty, tz = face_values(logk)
    den = storage + tx[:, 1:] + tx[:, :-1] + ty[:, :, 1:] + ty[:, :, :-1] + tz[1:] + tz[:-1]
    plane = NX * NY
    layer = wells // plane
    rest = wells % plane
    source = jnp.zeros(logk.shape, jnp.float32).at[layer, rest // NY, rest % NY].add(rates)
    hold = jnp.broadcast_to(fixed[None] != 0, logk.shape)
    steps_kept = []
    current = head0
    for step in range(STEPS):
        start = current
        iterates = [start]
        for sweep in range(SWEEPS):
            inner = neighbor_sum(tx, ty, tz, pad_plane(current))
            current = jnp.where(hold, start, (storage * start + source + inner) / den)
            iterates.append(current)
        steps_kept.append(iterates)

    def tangent(vector):
        dlk = jnp.sum(kweight * vector[support], axis=0)
        padded = jnp.pad(dlk, ((1, 1), (0, 0)))
        dtx = tx * (0.5 * (padded[1:] + padded[:-1]))[None]
        padded = jnp.pad(dlk, ((0, 0), (1, 1)))
        dty = ty * (0.5 * (padded[:, 1:] + padded[:, :-1]))[None]
        dtz = tz * dlk[None]
        dsum = dtx[:, 1:] + dtx[:, :-1] + dty[:, :, 1:] + dty[:, :, :-1] + dtz[1:] + dtz[:-1]
        dhead = jnp.zeros(logk.shape, jnp.float32)
        for iterates in steps_kept:
            dcur = dhead
            for sweep in range(SWEEPS):
                prev = iterates[sweep]
                new = iterates[sweep + 1]
                acc = neighbor_sum(dtx, dty, dtz, pad_plane(prev)) - new * dsum
                acc = acc + neighbor_sum(tx, ty, tz, pad_plane(dcur)) + storage * dhead
                dcur = jnp.where(hold, dhead, acc / den)
            dhead = dcur
        return dhead

    sensitivity = lax.map(tangent, directions)
    return current, sensitivity
```

```python
import jax
import jax.numpy as jnp
from jax import lax
from jax.experimental import pallas as pl
from jax.experimental.pallas import tpu as pltpu
from jax.sharding import PartitionSpec as P

SUB, LANE = 8, 128
LAYERS, ROWS, DIRS, SUPPORT = 4, 4, 4, 4
WIDE = 3 * ROWS
STEPS, SWEEPS = 2, 2
VERTICAL_RATIO = 0.3

LOGK, HEAD, DLK, STORE, FIXED = 0, 16, 32, 48, 60
PACKED = 63


def row_of(ref, lead, r):
    return ref[lead, pl.ds(r, SUB, stride=ROWS), :]


def gather_pack(logk, head, stor, fixed, supp, kwei, dirs, dlk, fw, bw, table):
    banks = dirs.shape[0] // DIRS
    for k in range(banks * DIRS):
        table[k] = jnp.broadcast_to(dirs[k : k + 1, :], (SUB, LANE))

    def row(r, carry):
        idx = [row_of(supp, s, r) for s in range(SUPPORT)]
        low = [i & (LANE - 1) for i in idx]
        high = [i >> 7 for i in idx]
        acc = [[jnp.zeros((SUB, LANE), jnp.float32) for _ in range(DIRS)] for _ in idx]
        for k in range(banks):
            hit = [h == k for h in high]
            for d in range(DIRS):
                t = table[k * DIRS + d]
                for s in range(SUPPORT):
                    g = jnp.take_along_axis(t, low[s], axis=1, mode="promise_in_bounds")
                    acc[s][d] = jnp.where(hit[s], g, acc[s][d])
        w = [row_of(kwei, s, r) for s in range(SUPPORT)]
        for d in range(DIRS):
            total = acc[0][d] * w[0]
            for s in range(1, SUPPORT):
                total = total + acc[s][d] * w[s]
            dlk[d * ROWS + r] = total
            fw[DLK + d * ROWS + r] = total
            bw[DLK + d * ROWS + r] = total
        return carry

    lax.fori_loop(0, ROWS, row, 0)
    for l in range(LAYERS):
        for r in range(ROWS):
            k = row_of(logk, l, r)
            fw[LOGK + l * ROWS + r] = k
            bw[LOGK + l * ROWS + r] = k
            h = row_of(head, l, r)
            fw[HEAD + l * ROWS + r] = h
            bw[HEAD + l * ROWS + r] = h
            s = row_of(stor, l, r)
            if r > 0:
                fw[STORE + l * 3 + r - 1] = s
            if r < 3:
                bw[STORE + l * 3 + r] = s
    for r in range(ROWS):
        f = fixed[pl.ds(r, SUB, stride=ROWS), :].astype(jnp.float32)
        if r > 0:
            fw[FIXED + r - 1] = f
        if r < 3:
            bw[FIXED + r] = f


def well_source(wells, rates, out):
    first = lax.axis_index("space") * ROWS - 3
    w = wells[...]
    layer = w >> 18
    x = ((w >> 10) & 255) - first
    chunk = (w >> 7) & 7
    inside = (x >= 0) & (x < 10)
    place = jnp.where(inside, (layer * 10 + x) * 8 + chunk, -1)
    count = w.shape[1]
    rows = out.shape[0]
    hit = lax.broadcasted_iota(jnp.int32, (rows, count), 0) == place
    left = jnp.where(hit, jnp.broadcast_to(rates[...], (rows, count)), 0.0)
    lane = lax.broadcasted_iota(jnp.int32, (LANE, count), 0) == (w & (LANE - 1))
    right = lane.astype(jnp.float32)
    out[...] = lax.dot_general(
        left,
        right,
        (((1,), (1,)), ((), ())),
        precision=lax.Precision.HIGHEST,
        preferred_element_type=jnp.float32,
    )


def sweeps_kernel(
    logk, head, stor, fixed, dlk, lft, rgt, src, head_out, sens_out,
    e, g0, g1, g2, g3, txp, txm, typ, tym, tzp, tzm, sc, sw, dl, dlp, dlm, d1, d2, d3,
):
    me = lax.axis_index("space")
    last = lax.axis_size("space") - 1
    keep_left = jnp.where(me > 0, 1.0, 0.0).astype(jnp.float32)
    keep_right = jnp.where(me < last, 1.0, 0.0).astype(jnp.float32)
    lanes = lax.broadcasted_iota(jnp.int32, (SUB, LANE), 1)
    subs = lax.broadcasted_iota(jnp.int32, (SUB, LANE), 0)
    lane_first, lane_last = lanes == 0, lanes == LANE - 1
    y_first = lane_first & (subs == 0)
    y_last = lane_last & (subs == SUB - 1)

    def up(v):
        return pltpu.roll(jnp.where(lane_first, pltpu.roll(v, SUB - 1, 0), v), LANE - 1, 1)

    def down(v):
        return pltpu.roll(jnp.where(lane_last, pltpu.roll(v, 1, 0), v), 1, 1)

    for l in range(LAYERS):
        for r in range(ROWS):
            i = l * ROWS + r
            e[l, r] = jnp.exp(0.5 * lft[LOGK + i])
            e[l, r + 4] = jnp.exp(0.5 * row_of(logk, l, r))
            e[l, r + 8] = jnp.exp(0.5 * rgt[LOGK + i])
            g0[l, r] = lft[HEAD + i]
            g0[l, r + 4] = row_of(head, l, r)
            g0[l, r + 8] = rgt[HEAD + i]
    for d in range(DIRS):
        for r in range(ROWS):
            i = d * ROWS + r
            dl[d, r] = 0.5 * lft[DLK + i]
            dl[d, r + 4] = 0.5 * dlk[i]
            dl[d, r + 8] = 0.5 * rgt[DLK + i]
    for d in range(DIRS):
        for r in range(1, WIDE - 1):
            v = dl[d, r]
            dlp[d, r] = up(v)
            dlm[d, r] = down(v)

    for r in range(1, WIDE - 1):
        if r < 4:
            hold = lft[FIXED + r - 1]
        elif r < 8:
            hold = fixed[pl.ds(r - 4, SUB, stride=ROWS), :].astype(jnp.float32)
        else:
            hold = rgt[FIXED + r - 8]
        held = hold > 0.5
        for l in range(LAYERS):
            if r < 4:
                st = lft[STORE + l * 3 + r - 1]
            elif r < 8:
                st = row_of(stor, l, r - 4)
            else:
                st = rgt[STORE + l * 3 + r - 8]
            c = e[l, r]
            xp, xm = c * e[l, r + 1], c * e[l, r - 1]
            if r == 3:
                xp = xp * keep_left
            if r == 4:
                xm = xm * keep_left
            if r == 7:
                xp = xp * keep_right
            if r == 8:
                xm = xm * keep_right
            yp = jnp.where(y_last, 0.0, c * up(c))
            ym = jnp.where(y_first, 0.0, c * down(c))
            den = st + xp + xm + yp + ym
            if l < LAYERS - 1:
                zp = VERTICAL_RATIO * (c * e[l + 1, r])
                den = den + zp
            if l > 0:
                zm = VERTICAL_RATIO * (c * e[l - 1, r])
                den = den + zm
            inv = 1.0 / den
            w = jnp.where(held, 0.0, inv)
            txp[l, r] = xp * w
            txm[l, r] = xm * w
            typ[l, r] = yp * w
            tym[l, r] = ym * w
            if l < LAYERS - 1:
                tzp[l, r] = zp * w
            if l > 0:
                tzm[l, r] = zm * w
            sc[l, r] = jnp.where(held, 1.0, st * inv)
            sw[l, r] = src[l * 10 + r - 1] * w

    def sweep(count, start, prev, new, dprev, dstart, dnew, r):
        for l in range(LAYERS):
            c = prev[l, r]
            pairs = [
                (txp[l, r], prev[l, r + 1]),
                (txm[l, r], prev[l, r - 1]),
                (typ[l, r], up(c)),
                (tym[l, r], down(c)),
            ]
            if l < LAYERS - 1:
                pairs.append((tzp[l, r], prev[l + 1, r]))
            if l > 0:
                pairs.append((tzm[l, r], prev[l - 1, r]))
            s = sc[l, r]
            value = s * start[l, r] + sw[l, r]
            for t, g in pairs:
                value = value + t * g
            if new is not None:
                new[l, r] = value
            else:
                head_out[l, pl.ds(r - 4, SUB, stride=ROWS), :] = value
            b = [t * (g - value) for t, g in pairs]
            flat = (b[0] + b[1]) + (b[2] + b[3])
            tall = b[4] + b[5] if len(b) == 6 else b[4]
            own = flat + (tall + tall)
            for d in range(DIRS):
                acc = own * dl[d, r] + b[0] * dl[d, r + 1] + b[1] * dl[d, r - 1]
                acc = acc + b[2] * dlp[d, r] + b[3] * dlm[d, r]
                if dprev is not None:
                    v = dprev[d, l, r]
                    acc = acc + pairs[0][0] * dprev[d, l, r + 1] + pairs[1][0] * dprev[d, l, r - 1]
                    acc = acc + pairs[2][0] * up(v) + pairs[3][0] * down(v)
                    n = 4
                    if l < LAYERS - 1:
                        acc = acc + pairs[n][0] * dprev[d, l + 1, r]
                        n += 1
                    if l > 0:
                        acc = acc + pairs[n][0] * dprev[d, l - 1, r]
                if dstart is not None:
                    acc = acc + s * dstart[d, l, r]
                if dnew is not None:
                    dnew[d, l, r] = acc
                else:
                    sens_out[d, l, pl.ds(r - 4, SUB, stride=ROWS), :] = acc

    def run(lo, hi, *what):
        def body(r, carry):
            sweep(0, *what, r)
            return carry

        lax.fori_loop(lo, hi, body, 0)

    run(1, 11, g0, g0, g1, None, None, d1)
    run(2, 10, g0, g1, g2, d1, None, d2)
    run(3, 9, g2, g2, g3, d2, d2, d3)
    for r in range(4, 8):
        sweep(0, g2, g3, None, d3, d2, None, r)


def tiles(x):
    lead, rows, width = x.shape
    x = x.reshape(lead, rows, width // LANE, LANE).transpose(0, 2, 1, 3)
    return x.reshape(lead, rows * width // LANE, LANE)


def rows_back(x, lead):
    x = x.reshape(*lead, SUB, ROWS, LANE)
    x = jnp.swapaxes(x, -3, -2)
    return x.reshape(*lead, ROWS, SUB * LANE)


def local(logk, storage, head0, support, kweight, fixed, directions, wells, rates):
    f32 = jnp.float32
    vmem = pl.BlockSpec(memory_space=pltpu.VMEM)
    logk, storage, head0, support, kweight = map(
        tiles, (logk, storage, head0, support, kweight)
    )
    fixed = tiles(fixed[None])[0]
    table = tiles(directions[None])[0]
    count = lax.axis_size("space")
    pack = jax.ShapeDtypeStruct((PACKED, SUB, LANE), f32)
    dlk, fw, bw = pl.pallas_call(
        gather_pack,
        out_shape=(jax.ShapeDtypeStruct((DIRS * ROWS, SUB, LANE), f32), pack, pack),
        in_specs=[vmem] * 7,
        out_specs=(vmem,) * 3,
        scratch_shapes=[pltpu.VMEM((table.shape[0], SUB, LANE), f32)],
        name="gather_pack",
    )(logk, head0, storage, fixed, support, kweight, table)
    lft = lax.ppermute(fw, "space", [(i, i + 1) for i in range(count - 1)])
    rgt = lax.ppermute(bw, "space", [(i + 1, i) for i in range(count - 1)])
    src = pl.pallas_call(
        well_source,
        out_shape=jax.ShapeDtypeStruct((LAYERS * 10 * SUB, LANE), f32),
        in_specs=[vmem] * 2,
        out_specs=vmem,
        name="well_source",
    )(wells[None], rates[None])
    src = src.reshape(LAYERS * 10, SUB, LANE)
    grid = pltpu.VMEM((LAYERS, WIDE, SUB, LANE), f32)
    field = pltpu.VMEM((DIRS, LAYERS, WIDE, SUB, LANE), f32)
    plane = pltpu.VMEM((DIRS, WIDE, SUB, LANE), f32)
    head, sens = pl.pallas_call(
        sweeps_kernel,
        out_shape=(
            jax.ShapeDtypeStruct((LAYERS, SUB * ROWS, LANE), f32),
            jax.ShapeDtypeStruct((DIRS, LAYERS, SUB * ROWS, LANE), f32),
        ),
        in_specs=[vmem] * 8,
        out_specs=(vmem, vmem),
        scratch_shapes=[grid] * 13 + [plane] * 3 + [field] * 3,
        name="sweeps",
    )(logk, head0, storage, fixed, dlk, lft, rgt, src)
    return rows_back(head, (LAYERS,)), rows_back(sens, (DIRS, LAYERS))


def solution(mesh):
    rows = P(None, "space", None)
    return jax.shard_map(
        local,
        mesh=mesh,
        in_specs=(rows,) * 5 + (P("space", None), P("dir", None), P(), P()),
        out_specs=(rows, P("dir", None, "space", None)),
        check_vma=False,
    )
```

```python
import jax
import jax.numpy as jnp
from jax import lax
from jax.experimental import pallas as pl
from jax.experimental.pallas import tpu as pltpu
from jax.sharding import PartitionSpec as P

SUB, LANE = 8, 128
LAYERS, ROWS, DIRS, SUPPORT = 4, 4, 4, 4
WIDE = 3 * ROWS
VERTICAL = 0.3
VMEM_BYTES = 16 * 2**20

LOGK, HEAD, DLK, STORE, FIXED, FULL = 0, 16, 32, 48, 64, 68
SENT_FIXED, NEAR, FAR = 60, 63, 64

GRID, PLANE, FIELD = LAYERS * WIDE, DIRS * WIDE, DIRS * LAYERS * WIDE
E, G0, G1, G2, G3, H0, H2, SC, PP, S0, SW = (i * GRID for i in range(11))
DL = 11 * GRID
DLU, DLD = DL + PLANE, DL + 2 * PLANE
KK = DL + 3 * PLANE
D1, D2, D3 = KK + FIELD, KK + 2 * FIELD, KK + 3 * FIELD
STATE = KK + 4 * FIELD


def tile(k):
    if isinstance(k, int):
        return pl.ds(k * SUB, SUB)
    return pl.ds(pl.multiple_of(k * SUB, SUB), SUB)


def odd():
    return lax.rem(lax.axis_index("space"), 2)


def gather_pack(*refs):
    hbm, (own, near, far), vmem, sem = refs[:7], refs[7:10], refs[10:17], refs[17]
    loads = [pltpu.make_async_copy(a, b, sem.at[i]) for i, (a, b) in enumerate(zip(hbm, vmem))]
    for load in loads[::-1]:
        load.start()
    logk, head, stor, fixed, supp, kwei, dirs = vmem
    p = odd()
    for load in loads[4:]:
        load.wait()

    def source_row(j):
        return jnp.where(p == 1, j, 3 - j)

    t = dirs[...]
    t_high = t.astype(jnp.bfloat16)
    t_low = (t - t_high.astype(jnp.float32)).astype(jnp.bfloat16)
    left = jnp.concatenate([t_high, t_low], axis=1)
    banks = dirs.shape[0] // DIRS
    places = lax.broadcasted_iota(jnp.int32, (LANE, LANE), 0).astype(jnp.bfloat16)
    half = lax.broadcasted_iota(jnp.int32, (SUB, LANE), 0) >> 2
    one, zero = jnp.bfloat16(1), jnp.bfloat16(0)

    def block(i, carry):
        j, pair = i >> 2, i & 3
        r = source_row(j)
        total = [None, None]
        for s in range(SUPPORT):
            hot, high, weight = [], [], []
            for h in range(2):
                at = (2 * pair + h) * ROWS + r
                idx = jnp.broadcast_to(supp[s, pl.ds(at, 1), :], (SUB, LANE))
                low = (idx & (LANE - 1)).astype(jnp.float32)
                low = jnp.concatenate([low, low], axis=0).astype(jnp.bfloat16)
                low = jnp.concatenate([low] * (LANE // 16), axis=0)
                hot.append(jnp.where(places == low, one, zero))
                high.append((idx >> 7) - half)
                weight.append(jnp.broadcast_to(kwei[s, pl.ds(at, 1), :], (SUB, LANE)))
            right = jnp.concatenate(hot, axis=1)
            right = jnp.concatenate([right, right], axis=0)
            found = jnp.dot(left, right, preferred_element_type=jnp.float32)
            for h in range(2):
                value = jnp.zeros((SUB, LANE), jnp.float32)
                for m in range(banks // 2):
                    part = found[m * SUB : (m + 1) * SUB, h * LANE : (h + 1) * LANE]
                    value = jnp.where(high[h] == 2 * m, part, value)
                value = value * weight[h]
                total[h] = value if total[h] is None else total[h] + value
        for h in range(2):
            done = (total[h] + pltpu.roll(total[h], 4, 0))[:DIRS]
            at = DLK * SUB + j * SUB + 2 * pair + h
            own[pl.ds(at, DIRS, stride=ROWS * SUB), :] = done
            near[pl.ds(at, DIRS, stride=ROWS * SUB), :] = done
            far[pl.ds(at, DIRS, stride=ROWS * SUB), :] = done
        return carry

    lax.fori_loop(0, 4 * ROWS, block, 0)
    for load in loads[:4]:
        load.wait()
    far[tile(NEAR), :] = jnp.zeros((SUB, LANE), jnp.float32)
    for j in range(ROWS):
        r = source_row(j)
        for l in range(LAYERS):
            rows = pl.ds(r, SUB, stride=ROWS)
            k = logk[l, rows, :]
            own[tile(LOGK + l * ROWS + j), :] = k
            near[tile(LOGK + l * ROWS + j), :] = k
            far[tile(LOGK + l * ROWS + j), :] = k
            h = head[l, rows, :]
            own[tile(HEAD + l * ROWS + j), :] = h
            near[tile(HEAD + l * ROWS + j), :] = h
            far[tile(HEAD + l * ROWS + j), :] = h
            s = stor[l, rows, :]
            own[tile(STORE + l * ROWS + j), :] = s
            if j > 0:
                far[tile(STORE + l * 3 + j - 1), :] = s
            if j < 3:
                near[tile(STORE + l * 3 + j), :] = s
        f = fixed[pl.ds(r, SUB, stride=ROWS), :].astype(jnp.float32)
        own[tile(FIXED + j), :] = f
        if j > 0:
            far[tile(SENT_FIXED + j - 1), :] = f
        if j < 3:
            near[tile(SENT_FIXED + j), :] = f


def well_source(wells_hbm, rates_hbm, out, wells, rates, sem):
    loads = [
        pltpu.make_async_copy(wells_hbm, wells, sem.at[0]),
        pltpu.make_async_copy(rates_hbm, rates, sem.at[1]),
    ]
    for load in loads:
        load.start()
    p = odd()
    for load in loads:
        load.wait()
    first = lax.axis_index("space") * ROWS
    w = wells[...]
    x = ((w >> 10) & 255) - first
    place = jnp.where(p == 1, 3 - x, x) + 3
    inside = (place >= 0) & (place < 10)
    place = jnp.where(inside, ((w >> 18) * 10 + place) * SUB + ((w >> 7) & 7), -1)
    count = w.shape[1]
    rows = out.shape[0]
    hit = lax.broadcasted_iota(jnp.int32, (rows, count), 0) == place
    left = jnp.where(hit, jnp.broadcast_to(rates[...], (rows, count)), 0.0)
    lane = lax.broadcasted_iota(jnp.int32, (LANE, count), 0) == (w & (LANE - 1))
    out[...] = lax.dot_general(
        left,
        lane.astype(jnp.float32),
        (((1,), (1,)), ((), ())),
        precision=lax.Precision.HIGHEST,
        preferred_element_type=jnp.float32,
    )


class Sweeper:
    def __init__(self, st, src):
        self.st, self.src = st, src
        lanes = lax.broadcasted_iota(jnp.int32, (SUB, LANE), 1)
        subs = lax.broadcasted_iota(jnp.int32, (SUB, LANE), 0)
        self.lane_first, self.lane_last = lanes == 0, lanes == LANE - 1
        self.sub_first, self.sub_last = subs == 0, subs == SUB - 1

    def get(self, base, i):
        return self.st[tile(base + i), :]

    def put(self, base, i, v):
        self.st[tile(base + i), :] = v

    def up(self, v):
        edge = jnp.where(self.sub_last, 0.0, pltpu.roll(v, SUB - 1, 0))
        return pltpu.roll(jnp.where(self.lane_first, edge, v), LANE - 1, 1)

    def down(self, v):
        edge = jnp.where(self.sub_first, 0.0, pltpu.roll(v, 1, 0))
        return pltpu.roll(jnp.where(self.lane_last, edge, v), 1, 1)

    def fill(self, pack, place, keep=None):
        for l in range(LAYERS):
            for j in range(ROWS):
                i = l * WIDE + place(j)
                e = jnp.exp(0.5 * pack[tile(LOGK + l * ROWS + j), :])
                if keep is not None:
                    e = e * keep
                h = pack[tile(HEAD + l * ROWS + j), :]
                self.put(E, i, e)
                self.put(G0, i, e * h)
                self.put(H0, i, h)
        for d in range(DIRS):
            for j in range(ROWS):
                i = d * WIDE + place(j)
                v = 0.5 * pack[tile(DLK + d * ROWS + j), :]
                self.put(DL, i, v)
                if 0 < place(j) < WIDE - 1:
                    self.put(DLU, i, self.up(v))
                    self.put(DLD, i, self.down(v))

    def coefficients(self, w, pack, store_at, fixed_at, missing=None):
        held = pack[tile(fixed_at), :] > 0.5
        dl = [[self.get(DL, d * WIDE + w + o) for o in (-1, 0, 1)] for d in range(DIRS)]
        dlu = [self.get(DLU, d * WIDE + w) for d in range(DIRS)]
        dld = [self.get(DLD, d * WIDE + w) for d in range(DIRS)]
        for l in range(LAYERS):
            i = l * WIDE + w
            e = self.get(E, i)
            xp, xm = self.get(E, i + 1), self.get(E, i - 1)
            yp, ym = self.up(e), self.down(e)
            tall = None
            if l < LAYERS - 1:
                tall = self.get(E, i + WIDE)
            if l > 0:
                below = self.get(E, i - WIDE)
                tall = below if tall is None else tall + below
            tall = VERTICAL * tall
            total = ((xp + xm) + (yp + ym)) + tall
            store = pack[tile(store_at(l)), :]
            if missing is not None:
                store = store + missing
            inv = 1.0 / (store + e * total)
            free = jnp.where(held, 0.0, inv)
            self.put(S0, i, total)
            self.put(PP, i, free * e)
            self.put(SC, i, jnp.where(held, 1.0, store * inv))
            self.put(SW, i, self.src[tile(l * 10 + w - 1), :] * free)
            for d in range(DIRS):
                k = xp * dl[d][2] + xm * dl[d][0] + yp * dlu[d] + ym * dld[d] + tall * dl[d][1]
                self.put(KK, (d * LAYERS + l) * WIDE + w, k)

    def sweep(self, number, w, outs=None):
        start = H0 if number < 3 else H2
        prev = (G0, G1, G2, G3)[number - 1]
        new = (G1, G2, G3, None)[number - 1]
        dprev = (None, D1, D2, D3)[number - 1]
        dnew = (D1, D2, D3, None)[number - 1]
        get = self.get
        dl = [[get(DL, d * WIDE + w + o) for o in (-1, 0, 1)] for d in range(DIRS)]
        dlu = [get(DLU, d * WIDE + w) for d in range(DIRS)]
        dld = [get(DLD, d * WIDE + w) for d in range(DIRS)]
        for l in range(LAYERS):
            i = l * WIDE + w
            here = get(prev, i)
            xp, xm = get(prev, i + 1), get(prev, i - 1)
            yp, ym = self.up(here), self.down(here)
            tall = None
            if l < LAYERS - 1:
                tall = get(prev, i + WIDE)
            if l > 0:
                below = get(prev, i - WIDE)
                tall = below if tall is None else tall + below
            tall = VERTICAL * tall
            total = ((xp + xm) + (yp + ym)) + tall
            e, sc, pp = get(E, i), get(SC, i), get(PP, i)
            value = sc * get(start, i) + get(SW, i) + pp * total
            if new is not None:
                self.put(new, i, e * value)
            if number == 2:
                self.put(H2, i, value)
            if outs is not None:
                outs[0][l, outs[2], :] = value
            own = (total - value * get(S0, i)) + tall
            scaled = pp if outs is not None else pp * e
            for d in range(DIRS):
                f = (d * LAYERS + l) * WIDE + w
                acc = own * dl[d][1] - value * get(KK, f)
                acc = acc + (xp * dl[d][2] + xm * dl[d][0])
                acc = acc + (yp * dlu[d] + ym * dld[d])
                if dprev is not None:
                    v = get(dprev, f)
                    acc = acc + (get(dprev, f + 1) + get(dprev, f - 1))
                    acc = acc + (self.up(v) + self.down(v))
                    side = None
                    if l < LAYERS - 1:
                        side = get(dprev, f + WIDE)
                    if l > 0:
                        below = get(dprev, f - WIDE)
                        side = below if side is None else side + below
                    acc = acc + VERTICAL * side
                out = scaled * acc
                if number == 3:
                    out = out + sc * get(D2, f)
                if dnew is not None:
                    self.put(dnew, f, out)
                else:
                    outs[1][d, l, outs[2], :] = out + (sc / e) * get(D2, f)

    def loop(self, number, lo, hi):
        def body(w, carry):
            self.sweep(number, w)
            return carry

        lax.fori_loop(lo, hi, body, 0)


def before_far(own, near, src, st):
    s = Sweeper(st, src)
    s.fill(own, lambda j: 7 - j)
    s.fill(near, lambda j: 8 + j)

    def own_row(w, carry):
        s.coefficients(w, own, lambda l: STORE + l * ROWS + 7 - w, FIXED + 7 - w)
        return carry

    def near_row(w, carry):
        s.coefficients(w, near, lambda l: STORE + l * 3 + w - 8, SENT_FIXED + w - 8)
        return carry

    lax.fori_loop(5, 8, own_row, 0)
    lax.fori_loop(8, 11, near_row, 0)
    s.loop(1, 5, 11)
    s.loop(2, 6, 10)
    s.loop(3, 7, 9)


def after_far(own, far, src, st_in, head_out, sens_out, st):
    del st_in
    me = lax.axis_index("space")
    inside = (me > 0) & (me < lax.axis_size("space") - 1)
    keep = jnp.where(inside, 1.0, 0.0).astype(jnp.float32)
    s = Sweeper(st, src)
    s.fill(far, lambda j: j, keep)

    def far_row(w, carry):
        s.coefficients(
            w, far, lambda l: STORE + l * 3 + w - 1, SENT_FIXED + w - 1, 1.0 - keep
        )
        return carry

    lax.fori_loop(1, 4, far_row, 0)
    s.coefficients(4, own, lambda l: STORE + l * ROWS + 3, FIXED + 3)
    s.loop(1, 1, 5)
    s.loop(2, 2, 6)
    s.loop(3, 3, 7)
    p = odd()

    def last(w, carry):
        r = jnp.where(p == 1, 7 - w, w - 4)
        s.sweep(4, w, (head_out, sens_out, pl.ds(r, SUB, stride=ROWS)))
        return carry

    lax.fori_loop(4, 8, last, 0)


def tiles(x):
    lead, rows, width = x.shape
    x = x.reshape(lead, rows, width // LANE, LANE).transpose(0, 2, 1, 3)
    return x.reshape(lead, rows * width // LANE, LANE)


def rows_back(x, lead):
    x = x.reshape(*lead, SUB, ROWS, LANE)
    x = jnp.swapaxes(x, -3, -2)
    return x.reshape(*lead, ROWS, SUB * LANE)


def local(logk, storage, head0, support, kweight, fixed, directions, wells, rates):
    f32 = jnp.float32
    vmem = pl.BlockSpec(memory_space=pltpu.VMEM)
    hbm = pl.BlockSpec(memory_space=pltpu.HBM)
    logk, storage, head0, support, kweight = map(
        tiles, (logk, storage, head0, support, kweight)
    )
    fixed = tiles(fixed[None])[0]
    table = tiles(directions[None])[0]
    inputs = [
        pltpu.with_memory_space_constraint(x, pltpu.HBM)
        for x in (logk, head0, storage, fixed, support, kweight, table)
    ]
    count = lax.axis_size("space")
    own, near, far = pl.pallas_call(
        gather_pack,
        out_shape=(
            pltpu.VMEM((FULL * SUB, LANE), f32),
            pltpu.VMEM((NEAR * SUB, LANE), f32),
            pltpu.VMEM((FAR * SUB, LANE), f32),
        ),
        in_specs=[hbm] * 7,
        out_specs=(vmem,) * 3,
        scratch_shapes=[pltpu.VMEM(x.shape, x.dtype) for x in inputs]
        + [pltpu.SemaphoreType.DMA((7,))],
        compiler_params=pltpu.CompilerParams(vmem_limit_bytes=VMEM_BYTES),
        name="gather_pack",
    )(*inputs)
    far = lax.ppermute(
        far,
        "space",
        [(i, i + 1 if i % 2 else i - 1) for i in range(1, count - 1)],
    )
    near = lax.ppermute(near, "space", [(i, i ^ 1) for i in range(count)])
    src = pl.pallas_call(
        well_source,
        out_shape=pltpu.VMEM((LAYERS * 10 * SUB, LANE), f32),
        in_specs=[hbm] * 2,
        out_specs=vmem,
        scratch_shapes=[
            pltpu.VMEM((1, wells.shape[0]), wells.dtype),
            pltpu.VMEM((1, rates.shape[0]), rates.dtype),
            pltpu.SemaphoreType.DMA((2,)),
        ],
        compiler_params=pltpu.CompilerParams(vmem_limit_bytes=VMEM_BYTES),
        name="well_source",
    )(*(pltpu.with_memory_space_constraint(x[None], pltpu.HBM) for x in (wells, rates)))
    state = pl.pallas_call(
        before_far,
        out_shape=pltpu.VMEM((STATE * SUB, LANE), f32),
        in_specs=[vmem] * 3,
        out_specs=vmem,
        compiler_params=pltpu.CompilerParams(vmem_limit_bytes=VMEM_BYTES),
        cost_estimate=pl.CostEstimate(flops=0, bytes_accessed=0, transcendentals=0),
        name="before_far",
    )(own, near, src)
    head, sens, _ = pl.pallas_call(
        after_far,
        out_shape=(
            jax.ShapeDtypeStruct((LAYERS, SUB * ROWS, LANE), f32),
            jax.ShapeDtypeStruct((DIRS, LAYERS, SUB * ROWS, LANE), f32),
            pltpu.VMEM((STATE * SUB, LANE), f32),
        ),
        in_specs=[vmem] * 4,
        out_specs=(vmem,) * 3,
        input_output_aliases={3: 2},
        compiler_params=pltpu.CompilerParams(vmem_limit_bytes=VMEM_BYTES),
        name="after_far",
    )(own, far, src, state)
    return rows_back(head, (LAYERS,)), rows_back(sens, (DIRS, LAYERS))


def solution(mesh):
    rows = P(None, "space", None)
    return jax.shard_map(
        local,
        mesh=mesh,
        in_specs=(rows,) * 5 + (P("space", None), P("dir", None), P(), P()),
        out_specs=(rows, P("dir", None, "space", None)),
        check_vma=False,
    )
```

```python
import jax
import jax.numpy as jnp
from jax import lax
from jax.experimental import pallas as pl
from jax.experimental.pallas import tpu as pltpu
from jax.sharding import PartitionSpec as P

SUB, LANE = 8, 128
LAYERS, ROWS, DIRS, SUPPORT = 4, 4, 4, 4
WIDE = 3 * ROWS
VERTICAL = 0.3
VMEM_BYTES = 16 * 2**20

LOGK, HEAD, DLK, STORE, FIXED, FULL = 0, 16, 32, 48, 64, 68
SENT_FIXED, NEAR, FAR = 60, 63, 64

GRID, PLANE, FIELD = LAYERS * WIDE, DIRS * WIDE, DIRS * LAYERS * WIDE
E, G0, G1, G2, G3, H0, H2, SC, PP, S0, SW = (i * GRID for i in range(11))
DL = 11 * GRID
DLU, DLD = DL + PLANE, DL + 2 * PLANE
KK = DL + 3 * PLANE
D1, D2, D3 = KK + FIELD, KK + 2 * FIELD, KK + 3 * FIELD
STATE = KK + 4 * FIELD


def tile(k):
    if isinstance(k, int):
        return pl.ds(k * SUB, SUB)
    return pl.ds(pl.multiple_of(k * SUB, SUB), SUB)


def odd():
    return lax.rem(lax.axis_index("space"), 2)


def gather_pack(*refs):
    hbm, (own, near, far), vmem, sem = refs[:7], refs[7:10], refs[10:17], refs[17]
    loads = [pltpu.make_async_copy(a, b, sem.at[i]) for i, (a, b) in enumerate(zip(hbm, vmem))]
    for load in loads[::-1]:
        load.start()
    logk, head, stor, fixed, supp, kwei, dirs = vmem
    p = odd()
    for load in loads[4:]:
        load.wait()

    def source_row(j):
        return jnp.where(p == 1, j, 3 - j)

    t = dirs[...]
    t_high = t.astype(jnp.bfloat16)
    t_low = (t - t_high.astype(jnp.float32)).astype(jnp.bfloat16)
    left = jnp.concatenate([t_high, t_low], axis=0)
    banks = dirs.shape[0] // DIRS
    places = lax.broadcasted_iota(jnp.int32, (LANE, LANE), 0).astype(jnp.bfloat16)
    half = lax.broadcasted_iota(jnp.int32, (SUB, LANE), 0) >> 2
    one, zero = jnp.bfloat16(1), jnp.bfloat16(0)

    def block(i, carry):
        j, pair = i >> 2, i & 3
        r = source_row(j)
        total = [None, None]
        for s in range(SUPPORT):
            hot, high, weight = [], [], []
            for h in range(2):
                at = (2 * pair + h) * ROWS + r
                idx = jnp.broadcast_to(supp[s, pl.ds(at, 1), :], (SUB, LANE))
                low = (idx & (LANE - 1)).astype(jnp.float32)
                low = jnp.concatenate([low, low], axis=0).astype(jnp.bfloat16)
                low = jnp.concatenate([low] * (LANE // 16), axis=0)
                hot.append(jnp.where(places == low, one, zero))
                high.append((idx >> 7) - half)
                weight.append(jnp.broadcast_to(kwei[s, pl.ds(at, 1), :], (SUB, LANE)))
            right = jnp.concatenate(hot, axis=1)
            found = jnp.dot(left, right, preferred_element_type=jnp.float32)
            found = found[: banks * DIRS] + found[banks * DIRS :]
            for h in range(2):
                value = jnp.zeros((SUB, LANE), jnp.float32)
                for m in range(banks // 2):
                    part = found[m * SUB : (m + 1) * SUB, h * LANE : (h + 1) * LANE]
                    value = jnp.where(high[h] == 2 * m, part, value)
                value = value * weight[h]
                total[h] = value if total[h] is None else total[h] + value
        for h in range(2):
            done = (total[h] + pltpu.roll(total[h], 4, 0))[:DIRS]
            at = DLK * SUB + j * SUB + 2 * pair + h
            own[pl.ds(at, DIRS, stride=ROWS * SUB), :] = done
            near[pl.ds(at, DIRS, stride=ROWS * SUB), :] = done
            far[pl.ds(at, DIRS, stride=ROWS * SUB), :] = done
        return carry

    lax.fori_loop(0, 4 * ROWS, block, 0, unroll=True)
    for load in loads[:4]:
        load.wait()
    far[tile(NEAR), :] = jnp.zeros((SUB, LANE), jnp.float32)
    for j in range(ROWS):
        r = source_row(j)
        for l in range(LAYERS):
            rows = pl.ds(r, SUB, stride=ROWS)
            k = logk[l, rows, :]
            own[tile(LOGK + l * ROWS + j), :] = k
            near[tile(LOGK + l * ROWS + j), :] = k
            far[tile(LOGK + l * ROWS + j), :] = k
            h = head[l, rows, :]
            own[tile(HEAD + l * ROWS + j), :] = h
            near[tile(HEAD + l * ROWS + j), :] = h
            far[tile(HEAD + l * ROWS + j), :] = h
            s = stor[l, rows, :]
            own[tile(STORE + l * ROWS + j), :] = s
            if j > 0:
                far[tile(STORE + l * 3 + j - 1), :] = s
            if j < 3:
                near[tile(STORE + l * 3 + j), :] = s
        f = fixed[pl.ds(r, SUB, stride=ROWS), :].astype(jnp.float32)
        own[tile(FIXED + j), :] = f
        if j > 0:
            far[tile(SENT_FIXED + j - 1), :] = f
        if j < 3:
            near[tile(SENT_FIXED + j), :] = f


def well_source(wells_hbm, rates_hbm, out, wells, rates, sem):
    loads = [
        pltpu.make_async_copy(wells_hbm, wells, sem.at[0]),
        pltpu.make_async_copy(rates_hbm, rates, sem.at[1]),
    ]
    for load in loads:
        load.start()
    p = odd()
    for load in loads:
        load.wait()
    first = lax.axis_index("space") * ROWS
    w = wells[...]
    x = ((w >> 10) & 255) - first
    place = jnp.where(p == 1, 3 - x, x) + 3
    inside = (place >= 0) & (place < 10)
    place = jnp.where(inside, ((w >> 18) * 10 + place) * SUB + ((w >> 7) & 7), -1)
    count = w.shape[1]
    rows = out.shape[0]
    hit = lax.broadcasted_iota(jnp.int32, (rows, count), 0) == place
    left = hit.astype(jnp.float32).astype(jnp.bfloat16)
    lane = lax.broadcasted_iota(jnp.int32, (LANE, count), 0) == (w & (LANE - 1))
    rest = rates[...]
    parts = []
    for _ in range(3):
        part = rest.astype(jnp.bfloat16).astype(jnp.float32)
        rest = rest - part
        parts.append(jnp.where(lane, part, 0.0).astype(jnp.bfloat16))
    total = lax.dot_general(
        left,
        jnp.concatenate(parts, axis=0),
        (((1,), (1,)), ((), ())),
        preferred_element_type=jnp.float32,
    )
    out[...] = (total[:, :LANE] + total[:, LANE : 2 * LANE]) + total[:, 2 * LANE :]


class Sweeper:
    def __init__(self, st, src):
        self.st, self.src = st, src
        lanes = lax.broadcasted_iota(jnp.int32, (SUB, LANE), 1)
        subs = lax.broadcasted_iota(jnp.int32, (SUB, LANE), 0)
        self.lane_first, self.lane_last = lanes == 0, lanes == LANE - 1
        self.sub_first, self.sub_last = subs == 0, subs == SUB - 1

    def get(self, base, i):
        return self.st[tile(base + i), :]

    def put(self, base, i, v):
        self.st[tile(base + i), :] = v

    def up(self, v):
        edge = jnp.where(self.sub_last, 0.0, pltpu.roll(v, SUB - 1, 0))
        return pltpu.roll(jnp.where(self.lane_first, edge, v), LANE - 1, 1)

    def down(self, v):
        edge = jnp.where(self.sub_first, 0.0, pltpu.roll(v, 1, 0))
        return pltpu.roll(jnp.where(self.lane_last, edge, v), 1, 1)

    def fill(self, pack, place, keep=None):
        for l in range(LAYERS):
            for j in range(ROWS):
                i = l * WIDE + place(j)
                e = jnp.exp(0.5 * pack[tile(LOGK + l * ROWS + j), :])
                if keep is not None:
                    e = e * keep
                h = pack[tile(HEAD + l * ROWS + j), :]
                self.put(E, i, e)
                self.put(G0, i, e * h)
                self.put(H0, i, h)
        for d in range(DIRS):
            for j in range(ROWS):
                i = d * WIDE + place(j)
                v = 0.5 * pack[tile(DLK + d * ROWS + j), :]
                self.put(DL, i, v)
                if 0 < place(j) < WIDE - 1:
                    self.put(DLU, i, self.up(v))
                    self.put(DLD, i, self.down(v))

    def coefficients(self, w, pack, store_at, fixed_at, missing=None):
        held = pack[tile(fixed_at), :] > 0.5
        dl = [[self.get(DL, d * WIDE + w + o) for o in (-1, 0, 1)] for d in range(DIRS)]
        dlu = [self.get(DLU, d * WIDE + w) for d in range(DIRS)]
        dld = [self.get(DLD, d * WIDE + w) for d in range(DIRS)]
        for l in range(LAYERS):
            i = l * WIDE + w
            e = self.get(E, i)
            xp, xm = self.get(E, i + 1), self.get(E, i - 1)
            yp, ym = self.up(e), self.down(e)
            tall = None
            if l < LAYERS - 1:
                tall = self.get(E, i + WIDE)
            if l > 0:
                below = self.get(E, i - WIDE)
                tall = below if tall is None else tall + below
            tall = VERTICAL * tall
            total = ((xp + xm) + (yp + ym)) + tall
            store = pack[tile(store_at(l)), :]
            if missing is not None:
                store = store + missing
            inv = 1.0 / (store + e * total)
            free = jnp.where(held, 0.0, inv)
            self.put(S0, i, total)
            self.put(PP, i, free * e)
            self.put(SC, i, jnp.where(held, 1.0, store * inv))
            self.put(SW, i, self.src[tile(l * 10 + w - 1), :] * free)
            for d in range(DIRS):
                k = xp * dl[d][2] + xm * dl[d][0] + yp * dlu[d] + ym * dld[d] + tall * dl[d][1]
                self.put(KK, (d * LAYERS + l) * WIDE + w, k)

    def sweep(self, number, w, outs=None):
        start = H0 if number < 3 else H2
        prev = (G0, G1, G2, G3)[number - 1]
        new = (G1, G2, G3, None)[number - 1]
        dprev = (None, D1, D2, D3)[number - 1]
        dnew = (D1, D2, D3, None)[number - 1]
        get = self.get
        dl = [[get(DL, d * WIDE + w + o) for o in (-1, 0, 1)] for d in range(DIRS)]
        dlu = [get(DLU, d * WIDE + w) for d in range(DIRS)]
        dld = [get(DLD, d * WIDE + w) for d in range(DIRS)]
        for l in range(LAYERS):
            i = l * WIDE + w
            here = get(prev, i)
            xp, xm = get(prev, i + 1), get(prev, i - 1)
            yp, ym = self.up(here), self.down(here)
            tall = None
            if l < LAYERS - 1:
                tall = get(prev, i + WIDE)
            if l > 0:
                below = get(prev, i - WIDE)
                tall = below if tall is None else tall + below
            tall = VERTICAL * tall
            total = ((xp + xm) + (yp + ym)) + tall
            e, sc, pp = get(E, i), get(SC, i), get(PP, i)
            value = sc * get(start, i) + get(SW, i) + pp * total
            if new is not None:
                self.put(new, i, e * value)
            if number == 2:
                self.put(H2, i, value)
            if outs is not None:
                outs[0][l, outs[2], :] = value
            own = (total - value * get(S0, i)) + tall
            scaled = pp if outs is not None else pp * e
            for d in range(DIRS):
                f = (d * LAYERS + l) * WIDE + w
                acc = own * dl[d][1] - value * get(KK, f)
                acc = acc + (xp * dl[d][2] + xm * dl[d][0])
                acc = acc + (yp * dlu[d] + ym * dld[d])
                if dprev is not None:
                    v = get(dprev, f)
                    acc = acc + (get(dprev, f + 1) + get(dprev, f - 1))
                    acc = acc + (self.up(v) + self.down(v))
                    side = None
                    if l < LAYERS - 1:
                        side = get(dprev, f + WIDE)
                    if l > 0:
                        below = get(dprev, f - WIDE)
                        side = below if side is None else side + below
                    acc = acc + VERTICAL * side
                out = scaled * acc
                if number == 3:
                    out = out + sc * get(D2, f)
                if dnew is not None:
                    self.put(dnew, f, out)
                else:
                    outs[1][d, l, outs[2], :] = out + (sc / e) * get(D2, f)

    def rows(self, number, lo, hi):
        for w in range(lo, hi):
            self.sweep(number, w)


def before_far(own, near, src, st):
    s = Sweeper(st, src)
    s.fill(own, lambda j: 7 - j)
    s.fill(near, lambda j: 8 + j)

    for w in range(5, 8):
        s.coefficients(w, own, lambda l: STORE + l * ROWS + 7 - w, FIXED + 7 - w)
    for w in range(8, 11):
        s.coefficients(w, near, lambda l: STORE + l * 3 + w - 8, SENT_FIXED + w - 8)
    s.rows(1, 5, 11)
    s.rows(2, 6, 10)
    s.rows(3, 7, 9)


def after_far(own, far, src, st_in, head_out, sens_out, st):
    del st_in
    me = lax.axis_index("space")
    inside = (me > 0) & (me < lax.axis_size("space") - 1)
    keep = jnp.where(inside, 1.0, 0.0).astype(jnp.float32)
    s = Sweeper(st, src)
    s.fill(far, lambda j: j, keep)

    for w in range(1, 4):
        s.coefficients(
            w, far, lambda l: STORE + l * 3 + w - 1, SENT_FIXED + w - 1, 1.0 - keep
        )
    s.coefficients(4, own, lambda l: STORE + l * ROWS + 3, FIXED + 3)
    s.rows(1, 1, 5)
    s.rows(2, 2, 6)
    s.rows(3, 3, 7)
    p = odd()
    for w in range(4, 8):
        r = jnp.where(p == 1, 7 - w, w - 4)
        s.sweep(4, w, (head_out, sens_out, pl.ds(r, SUB, stride=ROWS)))


def tiles(x):
    lead, rows, width = x.shape
    x = x.reshape(lead, rows, width // LANE, LANE).transpose(0, 2, 1, 3)
    return x.reshape(lead, rows * width // LANE, LANE)


def rows_back(x, lead):
    x = x.reshape(*lead, SUB, ROWS, LANE)
    x = jnp.swapaxes(x, -3, -2)
    return x.reshape(*lead, ROWS, SUB * LANE)


def local(logk, storage, head0, support, kweight, fixed, directions, wells, rates):
    f32 = jnp.float32
    vmem = pl.BlockSpec(memory_space=pltpu.VMEM)
    hbm = pl.BlockSpec(memory_space=pltpu.HBM)
    logk, storage, head0, support, kweight = map(
        tiles, (logk, storage, head0, support, kweight)
    )
    fixed = tiles(fixed[None])[0]
    table = tiles(directions[None])[0]
    inputs = [
        pltpu.with_memory_space_constraint(x, pltpu.HBM)
        for x in (logk, head0, storage, fixed, support, kweight, table)
    ]
    count = lax.axis_size("space")
    own, near, far = pl.pallas_call(
        gather_pack,
        out_shape=(
            pltpu.VMEM((FULL * SUB, LANE), f32),
            pltpu.VMEM((NEAR * SUB, LANE), f32),
            pltpu.VMEM((FAR * SUB, LANE), f32),
        ),
        in_specs=[hbm] * 7,
        out_specs=(vmem,) * 3,
        scratch_shapes=[pltpu.VMEM(x.shape, x.dtype) for x in inputs]
        + [pltpu.SemaphoreType.DMA((7,))],
        compiler_params=pltpu.CompilerParams(vmem_limit_bytes=VMEM_BYTES),
        name="gather_pack",
    )(*inputs)
    far = lax.ppermute(
        far,
        "space",
        [(i, i + 1 if i % 2 else i - 1) for i in range(1, count - 1)],
    )
    near = lax.ppermute(near, "space", [(i, i ^ 1) for i in range(count)])
    src = pl.pallas_call(
        well_source,
        out_shape=pltpu.VMEM((LAYERS * 10 * SUB, LANE), f32),
        in_specs=[hbm] * 2,
        out_specs=vmem,
        scratch_shapes=[
            pltpu.VMEM((1, wells.shape[0]), wells.dtype),
            pltpu.VMEM((1, rates.shape[0]), rates.dtype),
            pltpu.SemaphoreType.DMA((2,)),
        ],
        compiler_params=pltpu.CompilerParams(vmem_limit_bytes=VMEM_BYTES),
        name="well_source",
    )(*(pltpu.with_memory_space_constraint(x[None], pltpu.HBM) for x in (wells, rates)))
    state = pl.pallas_call(
        before_far,
        out_shape=pltpu.VMEM((STATE * SUB, LANE), f32),
        in_specs=[vmem] * 3,
        out_specs=vmem,
        compiler_params=pltpu.CompilerParams(vmem_limit_bytes=VMEM_BYTES),
        cost_estimate=pl.CostEstimate(flops=0, bytes_accessed=0, transcendentals=0),
        name="before_far",
    )(own, near, src)
    head, sens, _ = pl.pallas_call(
        after_far,
        out_shape=(
            jax.ShapeDtypeStruct((LAYERS, SUB * ROWS, LANE), f32),
            jax.ShapeDtypeStruct((DIRS, LAYERS, SUB * ROWS, LANE), f32),
            pltpu.VMEM((STATE * SUB, LANE), f32),
        ),
        in_specs=[vmem] * 4,
        out_specs=(vmem,) * 3,
        input_output_aliases={3: 2},
        compiler_params=pltpu.CompilerParams(vmem_limit_bytes=VMEM_BYTES),
        name="after_far",
    )(own, far, src, state)
    return rows_back(head, (LAYERS,)), rows_back(sens, (DIRS, LAYERS))


def solution(mesh):
    rows = P(None, "space", None)
    return jax.shard_map(
        local,
        mesh=mesh,
        in_specs=(rows,) * 5 + (P("space", None), P("dir", None), P(), P()),
        out_specs=(rows, P("dir", None, "space", None)),
        check_vma=False,
    )
```

```python
import jax
import jax.numpy as jnp
from jax import lax
from jax.experimental import pallas as pl
from jax.experimental.pallas import tpu as pltpu
from jax.sharding import PartitionSpec as P

SUB, LANE = 8, 128
LAYERS, ROWS, DIRS, SUPPORT = 4, 4, 4, 4
WIDE = 3 * ROWS
VERTICAL = 0.3
BY_LANES = 1
VMEM_BYTES = 16 * 2**20

LOGK, HEAD, DLK, STORE, FIXED, FULL = 0, 16, 32, 48, 64, 68
SENT_FIXED, NEAR, FAR = 60, 63, 64

GRID, PLANE, FIELD = LAYERS * WIDE, DIRS * WIDE, DIRS * LAYERS * WIDE
E, G0, G1, G2, G3, H0, H2, SC, PP, S0, SW = (i * GRID for i in range(11))
DL = 11 * GRID
DLU, DLD = DL + PLANE, DL + 2 * PLANE
KK = DL + 3 * PLANE
D1, D2, D3 = KK + FIELD, KK + 2 * FIELD, KK + 3 * FIELD
HALF = LAYERS + DIRS * LAYERS
EARLY = KK + 4 * FIELD
STATE = EARLY + 4 * HALF


def tile(k):
    if isinstance(k, int):
        return pl.ds(k * SUB, SUB)
    return pl.ds(pl.multiple_of(k * SUB, SUB), SUB)


def odd():
    return lax.rem(lax.axis_index("space"), 2)


def gather_pack(*refs):
    hbm, (own, near, far), vmem, sem = refs[:7], refs[7:10], refs[10:17], refs[17]
    loads = [pltpu.make_async_copy(a, b, sem.at[i]) for i, (a, b) in enumerate(zip(hbm, vmem))]
    for load in loads[::-1]:
        load.start()
    logk, head, stor, fixed, supp, kwei, dirs = vmem
    p = odd()
    for load in loads[4:]:
        load.wait()

    def source_row(j):
        return jnp.where(p == 1, j, 3 - j)

    t = dirs[...]
    t_high = t.astype(jnp.bfloat16)
    t_low = (t - t_high.astype(jnp.float32)).astype(jnp.bfloat16)
    left = jnp.concatenate([t_high, t_low], axis=0)
    banks = dirs.shape[0] // DIRS
    places = lax.broadcasted_iota(jnp.int32, (LANE, LANE), 0).astype(jnp.bfloat16)
    half = lax.broadcasted_iota(jnp.int32, (SUB, LANE), 0) >> 2
    one, zero = jnp.bfloat16(1), jnp.bfloat16(0)

    def block(i, carry):
        j, pair = i >> 2, i & 3
        r = source_row(j)
        total = [None, None]
        for s in range(SUPPORT):
            hot, high, weight = [], [], []
            for h in range(2):
                at = (2 * pair + h) * ROWS + r
                idx = jnp.broadcast_to(supp[s, pl.ds(at, 1), :], (SUB, LANE))
                low = (idx & (LANE - 1)).astype(jnp.float32)
                low = jnp.concatenate([low, low], axis=0).astype(jnp.bfloat16)
                low = jnp.concatenate([low] * (LANE // 16), axis=0)
                hot.append(jnp.where(places == low, one, zero))
                high.append((idx >> 7) - half)
                weight.append(jnp.broadcast_to(kwei[s, pl.ds(at, 1), :], (SUB, LANE)))
            right = jnp.concatenate(hot, axis=1)
            found = jnp.dot(left, right, preferred_element_type=jnp.float32)
            found = found[: banks * DIRS] + found[banks * DIRS :]
            for h in range(2):
                value = jnp.zeros((SUB, LANE), jnp.float32)
                for m in range(banks // 2):
                    part = found[m * SUB : (m + 1) * SUB, h * LANE : (h + 1) * LANE]
                    value = jnp.where(high[h] == 2 * m, part, value)
                value = value * weight[h]
                total[h] = value if total[h] is None else total[h] + value
        for h in range(2):
            done = (total[h] + pltpu.roll(total[h], 4, 0))[:DIRS]
            at = DLK * SUB + j * SUB + 2 * pair + h
            own[pl.ds(at, DIRS, stride=ROWS * SUB), :] = done
            near[pl.ds(at, DIRS, stride=ROWS * SUB), :] = done
            far[pl.ds(at, DIRS, stride=ROWS * SUB), :] = done
        return carry

    def by_lanes(j):
        r = source_row(j)
        rows = pl.ds(r, SUB, stride=ROWS)
        idx = [supp[s, rows, :] for s in range(SUPPORT)]
        low = [i & (LANE - 1) for i in idx]
        high = [i >> 7 for i in idx]
        found = [[jnp.zeros((SUB, LANE), jnp.float32)] * DIRS for _ in idx]
        for k in range(banks):
            hit = [h == k for h in high]
            for d in range(DIRS):
                bank = jnp.broadcast_to(dirs[pl.ds(k * DIRS + d, 1), :], (SUB, LANE))
                for s in range(SUPPORT):
                    g = jnp.take_along_axis(bank, low[s], axis=1, mode="promise_in_bounds")
                    found[s][d] = jnp.where(hit[s], g, found[s][d])
        weight = [kwei[s, rows, :] for s in range(SUPPORT)]
        for d in range(DIRS):
            total = found[0][d] * weight[0]
            for s in range(1, SUPPORT):
                total = total + found[s][d] * weight[s]
            for out in (own, near, far):
                out[tile(DLK + d * ROWS + j), :] = total

    for i in range(4 * ROWS):
        if i == 0:
            by_lanes(0)
        if i >= 4 * BY_LANES:
            block(i, 0)
    for load in loads[:4]:
        load.wait()
    far[tile(NEAR), :] = jnp.zeros((SUB, LANE), jnp.float32)
    for j in range(ROWS):
        r = source_row(j)
        for l in range(LAYERS):
            rows = pl.ds(r, SUB, stride=ROWS)
            k = logk[l, rows, :]
            own[tile(LOGK + l * ROWS + j), :] = k
            near[tile(LOGK + l * ROWS + j), :] = k
            far[tile(LOGK + l * ROWS + j), :] = k
            h = head[l, rows, :]
            own[tile(HEAD + l * ROWS + j), :] = h
            near[tile(HEAD + l * ROWS + j), :] = h
            far[tile(HEAD + l * ROWS + j), :] = h
            s = stor[l, rows, :]
            own[tile(STORE + l * ROWS + j), :] = s
            if j > 0:
                far[tile(STORE + l * 3 + j - 1), :] = s
            if j < 3:
                near[tile(STORE + l * 3 + j), :] = s
        f = fixed[pl.ds(r, SUB, stride=ROWS), :].astype(jnp.float32)
        own[tile(FIXED + j), :] = f
        if j > 0:
            far[tile(SENT_FIXED + j - 1), :] = f
        if j < 3:
            near[tile(SENT_FIXED + j), :] = f


def well_source(wells_hbm, rates_hbm, out, wells, rates, sem):
    loads = [
        pltpu.make_async_copy(wells_hbm, wells, sem.at[0]),
        pltpu.make_async_copy(rates_hbm, rates, sem.at[1]),
    ]
    for load in loads:
        load.start()
    p = odd()
    for load in loads:
        load.wait()
    first = lax.axis_index("space") * ROWS
    w = wells[...]
    x = ((w >> 10) & 255) - first
    place = jnp.where(p == 1, 3 - x, x) + 3
    inside = (place >= 0) & (place < 10)
    place = jnp.where(inside, ((w >> 18) * 10 + place) * SUB + ((w >> 7) & 7), -1)
    count = w.shape[1]
    rows = out.shape[0]
    hit = lax.broadcasted_iota(jnp.int32, (rows, count), 0) == place
    left = hit.astype(jnp.float32).astype(jnp.bfloat16)
    lane = lax.broadcasted_iota(jnp.int32, (LANE, count), 0) == (w & (LANE - 1))
    rest = rates[...]
    parts = []
    for _ in range(3):
        part = rest.astype(jnp.bfloat16).astype(jnp.float32)
        rest = rest - part
        parts.append(jnp.where(lane, part, 0.0).astype(jnp.bfloat16))
    total = lax.dot_general(
        left,
        jnp.concatenate(parts, axis=0),
        (((1,), (1,)), ((), ())),
        preferred_element_type=jnp.float32,
    )
    out[...] = (total[:, :LANE] + total[:, LANE : 2 * LANE]) + total[:, 2 * LANE :]


class Sweeper:
    def __init__(self, st, src):
        self.st, self.src = st, src
        lanes = lax.broadcasted_iota(jnp.int32, (SUB, LANE), 1)
        subs = lax.broadcasted_iota(jnp.int32, (SUB, LANE), 0)
        self.lane_first, self.lane_last = lanes == 0, lanes == LANE - 1
        self.sub_first, self.sub_last = subs == 0, subs == SUB - 1

    def get(self, base, i):
        return self.st[tile(base + i), :]

    def put(self, base, i, v):
        self.st[tile(base + i), :] = v

    def up(self, v):
        edge = jnp.where(self.sub_last, 0.0, pltpu.roll(v, SUB - 1, 0))
        return pltpu.roll(jnp.where(self.lane_first, edge, v), LANE - 1, 1)

    def down(self, v):
        edge = jnp.where(self.sub_first, 0.0, pltpu.roll(v, 1, 0))
        return pltpu.roll(jnp.where(self.lane_last, edge, v), 1, 1)

    def fill(self, pack, place, keep=None):
        for l in range(LAYERS):
            for j in range(ROWS):
                i = l * WIDE + place(j)
                e = jnp.exp(0.5 * pack[tile(LOGK + l * ROWS + j), :])
                if keep is not None:
                    e = e * keep
                h = pack[tile(HEAD + l * ROWS + j), :]
                self.put(E, i, e)
                self.put(G0, i, e * h)
                self.put(H0, i, h)
        for d in range(DIRS):
            for j in range(ROWS):
                i = d * WIDE + place(j)
                v = 0.5 * pack[tile(DLK + d * ROWS + j), :]
                self.put(DL, i, v)
                if 0 < place(j) < WIDE - 1:
                    self.put(DLU, i, self.up(v))
                    self.put(DLD, i, self.down(v))

    def coefficients(self, w, pack, store_at, fixed_at, missing=None):
        held = pack[tile(fixed_at), :] > 0.5
        dl = [[self.get(DL, d * WIDE + w + o) for o in (-1, 0, 1)] for d in range(DIRS)]
        dlu = [self.get(DLU, d * WIDE + w) for d in range(DIRS)]
        dld = [self.get(DLD, d * WIDE + w) for d in range(DIRS)]
        for l in range(LAYERS):
            i = l * WIDE + w
            e = self.get(E, i)
            xp, xm = self.get(E, i + 1), self.get(E, i - 1)
            yp, ym = self.up(e), self.down(e)
            tall = None
            if l < LAYERS - 1:
                tall = self.get(E, i + WIDE)
            if l > 0:
                below = self.get(E, i - WIDE)
                tall = below if tall is None else tall + below
            tall = VERTICAL * tall
            total = ((xp + xm) + (yp + ym)) + tall
            store = pack[tile(store_at(l)), :]
            if missing is not None:
                store = store + missing
            inv = 1.0 / (store + e * total)
            free = jnp.where(held, 0.0, inv)
            self.put(S0, i, total)
            self.put(PP, i, free * e)
            self.put(SC, i, jnp.where(held, 1.0, store * inv))
            self.put(SW, i, self.src[tile(l * 10 + w - 1), :] * free)
            for d in range(DIRS):
                k = xp * dl[d][2] + xm * dl[d][0] + yp * dlu[d] + ym * dld[d] + tall * dl[d][1]
                self.put(KK, (d * LAYERS + l) * WIDE + w, k)

    def base_sides(self, number, w):
        prev = (G0, G1, G2, G3)[number - 1]
        here = [self.get(prev, l * WIDE + w) for l in range(LAYERS)]
        return [
            (self.get(prev, l * WIDE + w + 1), self.up(g), self.down(g), self.tall(here, l))
            for l, g in enumerate(here)
        ]

    def tall(self, here, l):
        beside = [here[k] for k in (l - 1, l + 1) if 0 <= k < LAYERS]
        return VERTICAL * (beside[0] if len(beside) == 1 else beside[0] + beside[1])

    def tangent_sides(self, number, w, d, sides):
        dprev = (None, D1, D2, D3)[number - 1]
        p = d * WIDE + w
        here, after = self.get(DL, p), self.get(DL, p + 1)
        plus, minus = self.get(DLU, p), self.get(DLD, p)
        sums = [(xp * after + tall * here) + (yp * plus + ym * minus) for xp, yp, ym, tall in sides]
        if dprev is not None:
            at = [(d * LAYERS + l) * WIDE + w for l in range(LAYERS)]
            v = [self.get(dprev, f) for f in at]
            sums = [
                acc + ((self.up(v[l]) + self.down(v[l])) + (self.get(dprev, at[l] + 1) + self.tall(v, l)))
                for l, acc in enumerate(sums)
            ]
        return sums

    def early(self, number, w):
        at = (number - 1) * HALF
        sides = self.base_sides(number, w)
        for l, (xp, yp, ym, tall) in enumerate(sides):
            self.put(EARLY, at + l, (xp + tall) + (yp + ym))
        for d in range(DIRS):
            for l, acc in enumerate(self.tangent_sides(number, w, d, sides)):
                self.put(EARLY, at + LAYERS + d * LAYERS + l, acc)

    def base_row(self, number, w, late=False, out=None):
        start = H0 if number < 3 else H2
        prev = (G0, G1, G2, G3)[number - 1]
        new = (G1, G2, G3, None)[number - 1]
        get = self.get
        at = (number - 1) * HALF
        sides = None if late else self.base_sides(number, w)
        base = []
        for l in range(LAYERS):
            i = l * WIDE + w
            if late:
                total = get(EARLY, at + l)
            else:
                xp, yp, ym, tall = sides[l]
                total = (xp + tall) + (yp + ym)
            xm = get(prev, i - 1)
            total = total + xm
            e, sc, pp = get(E, i), get(SC, i), get(PP, i)
            value = sc * get(start, i) + get(SW, i) + pp * total
            if new is not None:
                self.put(new, i, e * value)
            if number == 2:
                self.put(H2, i, value)
            if out is not None:
                out[0][l, out[1], :] = value
            scaled, kept = (pp, sc / e) if out is not None else (pp * e, sc)
            base.append((xm, value, total - value * get(S0, i), scaled, kept))
        return sides, base

    def tangent_row(self, number, w, d, sides, base, out=None):
        dprev = (None, D1, D2, D3)[number - 1]
        dnew = (D1, D2, D3, None)[number - 1]
        get = self.get
        if sides is None:
            at = (number - 1) * HALF + LAYERS + d * LAYERS
            sums = [get(EARLY, at + l) for l in range(LAYERS)]
        else:
            sums = self.tangent_sides(number, w, d, sides)
        p = d * WIDE + w
        here, before = get(DL, p), get(DL, p - 1)
        for l, (xm, value, own, scaled, kept) in enumerate(base):
            f = (d * LAYERS + l) * WIDE + w
            acc = sums[l] + xm * before
            if dprev is not None:
                acc = acc + get(dprev, f - 1)
            acc = acc + (own * here - value * get(KK, f))
            result = scaled * acc
            if number > 2:
                result = result + kept * get(D2, f)
            if out is None:
                self.put(dnew, f, result)
            else:
                out[0][d, l, out[1], :] = result

    def sweep(self, number, w, late=False):
        sides, base = self.base_row(number, w, late)
        for d in range(DIRS):
            self.tangent_row(number, w, d, sides, base)

    def rows(self, number, lo, hi):
        for w in range(lo, hi):
            self.sweep(number, w)


def before_far(own, near, src, st):
    s = Sweeper(st, src)
    s.fill(own, lambda j: 7 - j)
    s.fill(near, lambda j: 8 + j)

    for w in range(5, 8):
        s.coefficients(w, own, lambda l: STORE + l * ROWS + 7 - w, FIXED + 7 - w)
    for w in range(8, 11):
        s.coefficients(w, near, lambda l: STORE + l * 3 + w - 8, SENT_FIXED + w - 8)
    s.rows(1, 5, 11)
    s.rows(2, 6, 10)
    s.rows(3, 7, 9)
    for number in range(1, 5):
        s.early(number, number + 3)


def after_far(own, far, src, st_in, head_out, sens_out, st, head, sens, sem):
    del st_in
    me = lax.axis_index("space")
    inside = (me > 0) & (me < lax.axis_size("space") - 1)
    keep = jnp.where(inside, 1.0, 0.0).astype(jnp.float32)
    s = Sweeper(st, src)
    s.fill(far, lambda j: j, keep)

    for w in range(1, 4):
        s.coefficients(
            w, far, lambda l: STORE + l * 3 + w - 1, SENT_FIXED + w - 1, 1.0 - keep
        )
    s.coefficients(4, own, lambda l: STORE + l * ROWS + 3, FIXED + 3)
    for number in range(1, 4):
        s.rows(number, number, number + 3)
        s.sweep(number, number + 3, late=True)
    p = odd()
    rows = {w: pl.ds(jnp.where(p == 1, 7 - w, w - 4), SUB, stride=ROWS) for w in range(4, 8)}
    base = {w: s.base_row(4, w, w == 7, (head, rows[w])) for w in rows}
    stores = [pltpu.make_async_copy(head, head_out, sem.at[DIRS])]
    stores[0].start()
    for d in range(DIRS):
        for w in rows:
            s.tangent_row(4, w, d, *base[w], (sens, rows[w]))
        stores.append(pltpu.make_async_copy(sens.at[d], sens_out.at[d], sem.at[d]))
        stores[-1].start()
    for store in stores:
        store.wait()


def tiles(x):
    lead, rows, width = x.shape
    x = x.reshape(lead, rows, width // LANE, LANE).transpose(0, 2, 1, 3)
    return x.reshape(lead, rows * width // LANE, LANE)


def rows_back(x, lead):
    x = x.reshape(*lead, SUB, ROWS, LANE)
    x = jnp.swapaxes(x, -3, -2)
    return x.reshape(*lead, ROWS, SUB * LANE)


def local(logk, storage, head0, support, kweight, fixed, directions, wells, rates):
    f32 = jnp.float32
    vmem = pl.BlockSpec(memory_space=pltpu.VMEM)
    hbm = pl.BlockSpec(memory_space=pltpu.HBM)
    logk, storage, head0, support, kweight = map(
        tiles, (logk, storage, head0, support, kweight)
    )
    fixed = tiles(fixed[None])[0]
    table = tiles(directions[None])[0]
    inputs = [
        pltpu.with_memory_space_constraint(x, pltpu.HBM)
        for x in (logk, head0, storage, fixed, support, kweight, table)
    ]
    count = lax.axis_size("space")
    own, near, far = pl.pallas_call(
        gather_pack,
        out_shape=(
            pltpu.VMEM((FULL * SUB, LANE), f32),
            pltpu.VMEM((NEAR * SUB, LANE), f32),
            pltpu.VMEM((FAR * SUB, LANE), f32),
        ),
        in_specs=[hbm] * 7,
        out_specs=(vmem,) * 3,
        scratch_shapes=[pltpu.VMEM(x.shape, x.dtype) for x in inputs]
        + [pltpu.SemaphoreType.DMA((7,))],
        compiler_params=pltpu.CompilerParams(vmem_limit_bytes=VMEM_BYTES),
        name="gather_pack",
    )(*inputs)
    far = lax.ppermute(
        far,
        "space",
        [(i, i + 1 if i % 2 else i - 1) for i in range(1, count - 1)],
    )
    near = lax.ppermute(near, "space", [(i, i ^ 1) for i in range(count)])
    src = pl.pallas_call(
        well_source,
        out_shape=pltpu.VMEM((LAYERS * 10 * SUB, LANE), f32),
        in_specs=[hbm] * 2,
        out_specs=vmem,
        scratch_shapes=[
            pltpu.VMEM((1, wells.shape[0]), wells.dtype),
            pltpu.VMEM((1, rates.shape[0]), rates.dtype),
            pltpu.SemaphoreType.DMA((2,)),
        ],
        compiler_params=pltpu.CompilerParams(vmem_limit_bytes=VMEM_BYTES),
        name="well_source",
    )(*(pltpu.with_memory_space_constraint(x[None], pltpu.HBM) for x in (wells, rates)))
    state = pl.pallas_call(
        before_far,
        out_shape=pltpu.VMEM((STATE * SUB, LANE), f32),
        in_specs=[vmem] * 3,
        out_specs=vmem,
        compiler_params=pltpu.CompilerParams(vmem_limit_bytes=VMEM_BYTES),
        cost_estimate=pl.CostEstimate(flops=0, bytes_accessed=0, transcendentals=0),
        name="before_far",
    )(own, near, src)
    head, sens, _ = pl.pallas_call(
        after_far,
        out_shape=(
            pltpu.HBM((LAYERS, SUB * ROWS, LANE), f32),
            pltpu.HBM((DIRS, LAYERS, SUB * ROWS, LANE), f32),
            pltpu.VMEM((STATE * SUB, LANE), f32),
        ),
        in_specs=[vmem] * 4,
        out_specs=(hbm, hbm, vmem),
        scratch_shapes=[
            pltpu.VMEM((LAYERS, SUB * ROWS, LANE), f32),
            pltpu.VMEM((DIRS, LAYERS, SUB * ROWS, LANE), f32),
            pltpu.SemaphoreType.DMA((DIRS + 1,)),
        ],
        input_output_aliases={3: 2},
        compiler_params=pltpu.CompilerParams(vmem_limit_bytes=VMEM_BYTES),
        name="after_far",
    )(own, far, src, state)
    return rows_back(head, (LAYERS,)), rows_back(sens, (DIRS, LAYERS))


def solution(mesh):
    rows = P(None, "space", None)
    return jax.shard_map(
        local,
        mesh=mesh,
        in_specs=(rows,) * 5 + (P("space", None), P("dir", None), P(), P()),
        out_specs=(rows, P("dir", None, "space", None)),
        check_vma=False,
    )
```

```python
import jax
import jax.numpy as jnp
from jax import lax
from jax.experimental import pallas as pl
from jax.experimental.pallas import tpu as pltpu
from jax.sharding import PartitionSpec as P

SUB, LANE = 8, 128
LAYERS, ROWS, DIRS, SUPPORT = 4, 4, 4, 4
WIDE = 3 * ROWS
VERTICAL = 0.3
BY_LANES = (4, 1, 0, 0)
VMEM_BYTES = 16 * 2**20

ROOT, HEAD, DLK, STORE, FIXED, FULL = 0, 16, 32, 48, 64, 68
SENT_FIXED, NEAR, FAR = 60, 63, 64

GRID, PLANE, FIELD = LAYERS * WIDE, DIRS * WIDE, DIRS * LAYERS * WIDE
E, G0, G1, G2, G3, H0, H2, SC, PP, S0, SW = (i * GRID for i in range(11))
DL = 11 * GRID
DLU, DLD = DL + PLANE, DL + 2 * PLANE
KK = DL + 3 * PLANE
D1, D2, D3 = KK + FIELD, KK + 2 * FIELD, KK + 3 * FIELD
HALF = LAYERS + DIRS * LAYERS
EARLY = KK + 4 * FIELD
RR = EARLY + 4 * HALF
STATE = RR + LAYERS * ROWS


def tile(k):
    if isinstance(k, int):
        return pl.ds(k * SUB, SUB)
    return pl.ds(pl.multiple_of(k * SUB, SUB), SUB)


def odd():
    return lax.rem(lax.axis_index("space"), 2)


def gather_pack(*refs):
    hbm, (own, near, far), vmem, sem = refs[:7], refs[7:10], refs[10:17], refs[17]
    loads = [pltpu.make_async_copy(a, b, sem.at[i]) for i, (a, b) in enumerate(zip(hbm, vmem))]
    for load in loads[::-1]:
        load.start()
    logk, head, stor, fixed, supp, kwei, dirs = vmem
    p = odd()
    for load in loads[4:]:
        load.wait()

    def source_row(j):
        return jnp.where(p == 1, j, 3 - j)

    t = dirs[...]
    t_high = t.astype(jnp.bfloat16)
    t_low = (t - t_high.astype(jnp.float32)).astype(jnp.bfloat16)
    left = jnp.concatenate([t_high, t_low], axis=0)
    banks = dirs.shape[0] // DIRS
    places = lax.broadcasted_iota(jnp.int32, (LANE, LANE), 0).astype(jnp.bfloat16)
    half = lax.broadcasted_iota(jnp.int32, (SUB, LANE), 0) >> 2
    one, zero = jnp.bfloat16(1), jnp.bfloat16(0)

    def block(j, pair):
        r = source_row(j)
        total = [None, None]
        for s in range(BY_LANES[j], SUPPORT):
            hot, high, weight = [], [], []
            for h in range(2):
                at = (2 * pair + h) * ROWS + r
                idx = jnp.broadcast_to(supp[s, pl.ds(at, 1), :], (SUB, LANE))
                low = (idx & (LANE - 1)).astype(jnp.float32)
                low = jnp.concatenate([low, low], axis=0).astype(jnp.bfloat16)
                low = jnp.concatenate([low] * (LANE // 16), axis=0)
                hot.append(jnp.where(places == low, one, zero))
                high.append((idx >> 7) - half)
                weight.append(jnp.broadcast_to(kwei[s, pl.ds(at, 1), :], (SUB, LANE)))
            right = jnp.concatenate(hot, axis=1)
            found = jnp.dot(left, right, preferred_element_type=jnp.float32)
            found = found[: banks * DIRS] + found[banks * DIRS :]
            for h in range(2):
                value = jnp.zeros((SUB, LANE), jnp.float32)
                for m in range(banks // 2):
                    part = found[m * SUB : (m + 1) * SUB, h * LANE : (h + 1) * LANE]
                    value = jnp.where(high[h] == 2 * m, part, value)
                value = value * weight[h]
                total[h] = value if total[h] is None else total[h] + value
        for h in range(2):
            done = (0.5 * (total[h] + pltpu.roll(total[h], 4, 0)))[:DIRS]
            at = DLK * SUB + j * SUB + 2 * pair + h
            for out in (own, near, far) if BY_LANES[j] == 0 else (own,):
                out[pl.ds(at, DIRS, stride=ROWS * SUB), :] = done

    def by_lanes(j):
        r = source_row(j)
        rows = pl.ds(r, SUB, stride=ROWS)
        count = BY_LANES[j]
        idx = [supp[s, rows, :] for s in range(count)]
        low = [i & (LANE - 1) for i in idx]
        high = [i >> 7 for i in idx]
        found = [[jnp.zeros((SUB, LANE), jnp.float32)] * DIRS for _ in idx]
        for k in range(banks):
            hit = [h == k for h in high]
            for d in range(DIRS):
                bank = jnp.broadcast_to(dirs[pl.ds(k * DIRS + d, 1), :], (SUB, LANE))
                for s in range(count):
                    g = jnp.take_along_axis(bank, low[s], axis=1, mode="promise_in_bounds")
                    found[s][d] = jnp.where(hit[s], g, found[s][d])
        weight = [0.5 * kwei[s, rows, :] for s in range(count)]
        totals = []
        for d in range(DIRS):
            total = found[0][d] * weight[0]
            for s in range(1, count):
                total = total + found[s][d] * weight[s]
            totals.append(total)
        return totals

    def pack():
        far[tile(NEAR), :] = jnp.zeros((SUB, LANE), jnp.float32)
        for j in range(ROWS):
            r = source_row(j)
            rows = pl.ds(r, SUB, stride=ROWS)
            for l in range(LAYERS):
                k = jnp.exp(0.5 * logk[l, rows, :])
                h = head[l, rows, :]
                for out in (own, near, far):
                    out[tile(ROOT + l * ROWS + j), :] = k
                    out[tile(HEAD + l * ROWS + j), :] = h
                s = stor[l, rows, :]
                own[tile(STORE + l * ROWS + j), :] = s
                if j > 0:
                    far[tile(STORE + l * 3 + j - 1), :] = s
                if j < 3:
                    near[tile(STORE + l * 3 + j), :] = s
            f = fixed[rows, :].astype(jnp.float32)
            own[tile(FIXED + j), :] = f
            if j > 0:
                far[tile(SENT_FIXED + j - 1), :] = f
            if j < 3:
                near[tile(SENT_FIXED + j), :] = f

    lanes = {j: by_lanes(j) for j in range(ROWS) if BY_LANES[j]}
    for j in range(ROWS):
        if BY_LANES[j] < SUPPORT:
            for pair in range(4):
                block(j, pair)
        if BY_LANES[j]:
            for d in range(DIRS):
                at = tile(DLK + d * ROWS + j)
                value = lanes[j][d]
                if BY_LANES[j] < SUPPORT:
                    value = value + own[at, :]
                for out in (own, near, far):
                    out[at, :] = value
    for load in loads[:4]:
        load.wait()
    pack()


def well_source(wells_hbm, rates_hbm, out, wells, rates, sem):
    loads = [
        pltpu.make_async_copy(wells_hbm, wells, sem.at[0]),
        pltpu.make_async_copy(rates_hbm, rates, sem.at[1]),
    ]
    for load in loads:
        load.start()
    p = odd()
    for load in loads:
        load.wait()
    first = lax.axis_index("space") * ROWS
    w = wells[...]
    x = ((w >> 10) & 255) - first
    place = jnp.where(p == 1, 3 - x, x) + 3
    inside = (place >= 0) & (place < 10)
    place = jnp.where(inside, ((w >> 18) * 10 + place) * SUB + ((w >> 7) & 7), -1)
    count = w.shape[1]
    rows = out.shape[0]
    hit = lax.broadcasted_iota(jnp.int32, (rows, count), 0) == place
    left = hit.astype(jnp.float32).astype(jnp.bfloat16)
    lane = lax.broadcasted_iota(jnp.int32, (LANE, count), 0) == (w & (LANE - 1))
    rest = rates[...]
    parts = []
    for _ in range(3):
        part = rest.astype(jnp.bfloat16).astype(jnp.float32)
        rest = rest - part
        parts.append(jnp.where(lane, part, 0.0).astype(jnp.bfloat16))
    total = lax.dot_general(
        left,
        jnp.concatenate(parts, axis=0),
        (((1,), (1,)), ((), ())),
        preferred_element_type=jnp.float32,
    )
    out[...] = (total[:, :LANE] + total[:, LANE : 2 * LANE]) + total[:, 2 * LANE :]


class Sweeper:
    def __init__(self, st, src):
        self.st, self.src = st, src
        lanes = lax.broadcasted_iota(jnp.int32, (SUB, LANE), 1)
        subs = lax.broadcasted_iota(jnp.int32, (SUB, LANE), 0)
        self.lane_first, self.lane_last = lanes == 0, lanes == LANE - 1
        self.sub_first, self.sub_last = subs == 0, subs == SUB - 1

    def get(self, base, i):
        return self.st[tile(base + i), :]

    def put(self, base, i, v):
        self.st[tile(base + i), :] = v

    def up(self, v):
        edge = jnp.where(self.sub_last, 0.0, pltpu.roll(v, SUB - 1, 0))
        return pltpu.roll(jnp.where(self.lane_first, edge, v), LANE - 1, 1)

    def down(self, v):
        edge = jnp.where(self.sub_first, 0.0, pltpu.roll(v, 1, 0))
        return pltpu.roll(jnp.where(self.lane_last, edge, v), 1, 1)

    def fill(self, pack, place):
        for l in range(LAYERS):
            for j in range(ROWS):
                i = l * WIDE + place(j)
                e = pack[tile(ROOT + l * ROWS + j), :]
                h = pack[tile(HEAD + l * ROWS + j), :]
                self.put(E, i, e)
                self.put(G0, i, e * h)
                self.put(H0, i, h)
        for d in range(DIRS):
            for j in range(ROWS):
                i = d * WIDE + place(j)
                v = pack[tile(DLK + d * ROWS + j), :]
                self.put(DL, i, v)
                if 0 < place(j) < WIDE - 1:
                    self.put(DLU, i, self.up(v))
                    self.put(DLD, i, self.down(v))

    def coefficients(self, w, pack, store_at, fixed_at, missing=None):
        held = pack[tile(fixed_at), :] > 0.5
        dl = [[self.get(DL, d * WIDE + w + o) for o in (-1, 0, 1)] for d in range(DIRS)]
        dlu = [self.get(DLU, d * WIDE + w) for d in range(DIRS)]
        dld = [self.get(DLD, d * WIDE + w) for d in range(DIRS)]
        for l in range(LAYERS):
            i = l * WIDE + w
            e = self.get(E, i)
            xp, xm = self.get(E, i + 1), self.get(E, i - 1)
            yp, ym = self.up(e), self.down(e)
            tall = None
            if l < LAYERS - 1:
                tall = self.get(E, i + WIDE)
            if l > 0:
                below = self.get(E, i - WIDE)
                tall = below if tall is None else tall + below
            tall = VERTICAL * tall
            total = ((xp + xm) + (yp + ym)) + tall
            store = pack[tile(store_at(l)), :]
            if missing is not None:
                store = store + missing
            inv = 1.0 / (store + e * total)
            free = jnp.where(held, 0.0, inv)
            self.put(S0, i, total)
            self.put(PP, i, free * e)
            self.put(SC, i, jnp.where(held, 1.0, store * inv))
            self.put(SW, i, self.src[tile(l * 10 + w - 1), :] * free)
            for d in range(DIRS):
                k = xp * dl[d][2] + xm * dl[d][0] + yp * dlu[d] + ym * dld[d] + tall * dl[d][1]
                self.put(KK, (d * LAYERS + l) * WIDE + w, k)

    def base_sides(self, number, w):
        prev = (G0, G1, G2, G3)[number - 1]
        here = [self.get(prev, l * WIDE + w) for l in range(LAYERS)]
        return [
            (self.get(prev, l * WIDE + w + 1), self.up(g), self.down(g), self.tall(here, l))
            for l, g in enumerate(here)
        ]

    def tall(self, here, l):
        beside = [here[k] for k in (l - 1, l + 1) if 0 <= k < LAYERS]
        return VERTICAL * (beside[0] if len(beside) == 1 else beside[0] + beside[1])

    def tangent_sides(self, number, w, d, sides):
        dprev = (None, D1, D2, D3)[number - 1]
        p = d * WIDE + w
        here, after = self.get(DL, p), self.get(DL, p + 1)
        plus, minus = self.get(DLU, p), self.get(DLD, p)
        sums = [(xp * after + tall * here) + (yp * plus + ym * minus) for xp, yp, ym, tall in sides]
        if dprev is not None:
            at = [(d * LAYERS + l) * WIDE + w for l in range(LAYERS)]
            v = [self.get(dprev, f) for f in at]
            sums = [
                acc + ((self.up(v[l]) + self.down(v[l])) + (self.get(dprev, at[l] + 1) + self.tall(v, l)))
                for l, acc in enumerate(sums)
            ]
        return sums

    def early(self, number, w):
        at = (number - 1) * HALF
        sides = self.base_sides(number, w)
        for l, (xp, yp, ym, tall) in enumerate(sides):
            self.put(EARLY, at + l, (xp + tall) + (yp + ym))
        for d in range(DIRS):
            for l, acc in enumerate(self.tangent_sides(number, w, d, sides)):
                self.put(EARLY, at + LAYERS + d * LAYERS + l, acc)

    def base_row(self, number, w, late=False, out=None):
        start = H0 if number < 3 else H2
        prev = (G0, G1, G2, G3)[number - 1]
        new = (G1, G2, G3, None)[number - 1]
        get = self.get
        at = (number - 1) * HALF
        sides = None if late else self.base_sides(number, w)
        base = []
        for l in range(LAYERS):
            i = l * WIDE + w
            if late:
                total = get(EARLY, at + l)
            else:
                xp, yp, ym, tall = sides[l]
                total = (xp + tall) + (yp + ym)
            xm = get(prev, i - 1)
            total = total + xm
            e, sc, pp = get(E, i), get(SC, i), get(PP, i)
            value = sc * get(start, i) + get(SW, i) + pp * total
            if new is not None:
                self.put(new, i, e * value)
            if number == 2:
                self.put(H2, i, value)
            if out is not None:
                out[0][l, out[1], :] = value
            scaled, kept = pp * e, sc
            if out is not None:
                scaled, kept = pp, sc * get(RR, l * ROWS + w - 4)
            base.append((xm, value, total - value * get(S0, i), scaled, kept))
        return sides, base

    def tangent_row(self, number, w, d, sides, base, out=None):
        dprev = (None, D1, D2, D3)[number - 1]
        dnew = (D1, D2, D3, None)[number - 1]
        get = self.get
        if sides is None:
            at = (number - 1) * HALF + LAYERS + d * LAYERS
            sums = [get(EARLY, at + l) for l in range(LAYERS)]
        else:
            sums = self.tangent_sides(number, w, d, sides)
        p = d * WIDE + w
        here, before = get(DL, p), get(DL, p - 1)
        for l, (xm, value, own, scaled, kept) in enumerate(base):
            f = (d * LAYERS + l) * WIDE + w
            acc = sums[l] + xm * before
            if dprev is not None:
                acc = acc + get(dprev, f - 1)
            acc = acc + (own * here - value * get(KK, f))
            result = scaled * acc
            if number > 2:
                result = result + kept * get(D2, f)
            if out is None:
                self.put(dnew, f, result)
            else:
                out[0][d, l, out[1], :] = result

    def sweep(self, number, w, late=False):
        sides, base = self.base_row(number, w, late)
        for d in range(DIRS):
            self.tangent_row(number, w, d, sides, base)

    def rows(self, number, lo, hi):
        for w in range(lo, hi):
            self.sweep(number, w)


def before_far(own, near, src, st):
    s = Sweeper(st, src)
    s.fill(own, lambda j: 7 - j)
    s.fill(near, lambda j: 8 + j)

    for w in range(5, 8):
        s.coefficients(w, own, lambda l: STORE + l * ROWS + 7 - w, FIXED + 7 - w)
    for w in range(8, 11):
        s.coefficients(w, near, lambda l: STORE + l * 3 + w - 8, SENT_FIXED + w - 8)
    s.rows(1, 5, 11)
    s.rows(2, 6, 10)
    s.rows(3, 7, 9)
    for i in range(LAYERS * ROWS):
        l, w = divmod(i, ROWS)
        s.put(RR, i, 1.0 / s.get(E, l * WIDE + w + 4))
    for number in range(1, 5):
        s.early(number, number + 3)


def after_far(own, far, src, st_in, head_out, sens_out, st, head, sens, sem):
    del st_in
    me = lax.axis_index("space")
    inside = (me > 0) & (me < lax.axis_size("space") - 1)
    missing = jnp.where(inside, 0.0, 1.0).astype(jnp.float32)
    s = Sweeper(st, src)
    s.fill(far, lambda j: j)

    for w in range(1, 4):
        s.coefficients(
            w, far, lambda l: STORE + l * 3 + w - 1, SENT_FIXED + w - 1, missing
        )
    s.coefficients(4, own, lambda l: STORE + l * ROWS + 3, FIXED + 3)
    for number in range(1, 4):
        for w in range(number + 3, number - 1, -1):
            s.sweep(number, w, late=w == number + 3)
    p = odd()
    rows = {w: pl.ds(jnp.where(p == 1, 7 - w, w - 4), SUB, stride=ROWS) for w in range(4, 8)}
    base = {w: s.base_row(4, w, w == 7, (head, rows[w])) for w in rows}
    stores = [pltpu.make_async_copy(head, head_out, sem.at[DIRS])]
    stores[0].start()
    for d in range(DIRS):
        for w in (5, 6, 7, 4):
            s.tangent_row(4, w, d, *base[w], (sens, rows[w]))
        stores.append(pltpu.make_async_copy(sens.at[d], sens_out.at[d], sem.at[d]))
        stores[-1].start()
    for store in stores:
        store.wait()


def tiles(x):
    lead, rows, width = x.shape
    x = x.reshape(lead, rows, width // LANE, LANE).transpose(0, 2, 1, 3)
    return x.reshape(lead, rows * width // LANE, LANE)


def rows_back(x, lead):
    x = x.reshape(*lead, SUB, ROWS, LANE)
    x = jnp.swapaxes(x, -3, -2)
    return x.reshape(*lead, ROWS, SUB * LANE)


def local(logk, storage, head0, support, kweight, fixed, directions, wells, rates):
    f32 = jnp.float32
    vmem = pl.BlockSpec(memory_space=pltpu.VMEM)
    hbm = pl.BlockSpec(memory_space=pltpu.HBM)
    logk, storage, head0, support, kweight = map(
        tiles, (logk, storage, head0, support, kweight)
    )
    fixed = tiles(fixed[None])[0]
    table = tiles(directions[None])[0]
    inputs = [
        pltpu.with_memory_space_constraint(x, pltpu.HBM)
        for x in (logk, head0, storage, fixed, support, kweight, table)
    ]
    count = lax.axis_size("space")
    own, near, far = pl.pallas_call(
        gather_pack,
        out_shape=(
            pltpu.VMEM((FULL * SUB, LANE), f32),
            pltpu.VMEM((NEAR * SUB, LANE), f32),
            pltpu.VMEM((FAR * SUB, LANE), f32),
        ),
        in_specs=[hbm] * 7,
        out_specs=(vmem,) * 3,
        scratch_shapes=[pltpu.VMEM(x.shape, x.dtype) for x in inputs]
        + [pltpu.SemaphoreType.DMA((7,))],
        compiler_params=pltpu.CompilerParams(vmem_limit_bytes=VMEM_BYTES),
        name="gather_pack",
    )(*inputs)
    far = lax.ppermute(
        far,
        "space",
        [(i, i + 1 if i % 2 else i - 1) for i in range(1, count - 1)],
    )
    near = lax.ppermute(near, "space", [(i, i ^ 1) for i in range(count)])
    src = pl.pallas_call(
        well_source,
        out_shape=pltpu.VMEM((LAYERS * 10 * SUB, LANE), f32),
        in_specs=[hbm] * 2,
        out_specs=vmem,
        scratch_shapes=[
            pltpu.VMEM((1, wells.shape[0]), wells.dtype),
            pltpu.VMEM((1, rates.shape[0]), rates.dtype),
            pltpu.SemaphoreType.DMA((2,)),
        ],
        compiler_params=pltpu.CompilerParams(vmem_limit_bytes=VMEM_BYTES),
        name="well_source",
    )(*(pltpu.with_memory_space_constraint(x[None], pltpu.HBM) for x in (wells, rates)))
    state = pl.pallas_call(
        before_far,
        out_shape=pltpu.VMEM((STATE * SUB, LANE), f32),
        in_specs=[vmem] * 3,
        out_specs=vmem,
        compiler_params=pltpu.CompilerParams(vmem_limit_bytes=VMEM_BYTES),
        cost_estimate=pl.CostEstimate(flops=0, bytes_accessed=0, transcendentals=0),
        name="before_far",
    )(own, near, src)
    head, sens, _ = pl.pallas_call(
        after_far,
        out_shape=(
            pltpu.HBM((LAYERS, SUB * ROWS, LANE), f32),
            pltpu.HBM((DIRS, LAYERS, SUB * ROWS, LANE), f32),
            pltpu.VMEM((STATE * SUB, LANE), f32),
        ),
        in_specs=[vmem] * 4,
        out_specs=(hbm, hbm, vmem),
        scratch_shapes=[
            pltpu.VMEM((LAYERS, SUB * ROWS, LANE), f32),
            pltpu.VMEM((DIRS, LAYERS, SUB * ROWS, LANE), f32),
            pltpu.SemaphoreType.DMA((DIRS + 1,)),
        ],
        input_output_aliases={3: 2},
        compiler_params=pltpu.CompilerParams(vmem_limit_bytes=VMEM_BYTES),
        name="after_far",
    )(own, far, src, state)
    return rows_back(head, (LAYERS,)), rows_back(sens, (DIRS, LAYERS))


def solution(mesh):
    rows = P(None, "space", None)
    return jax.shard_map(
        local,
        mesh=mesh,
        in_specs=(rows,) * 5 + (P("space", None), P("dir", None), P(), P()),
        out_specs=(rows, P("dir", None, "space", None)),
        check_vma=False,
    )
```

```python
import jax
import jax.numpy as jnp
from jax import lax
from jax.experimental import pallas as pl
from jax.experimental.pallas import tpu as pltpu
from jax.sharding import PartitionSpec as P

SUB, LANE = 8, 128
LAYERS, ROWS, DIRS, SUPPORT = 4, 4, 4, 4
WIDE = 3 * ROWS
VERTICAL = 0.3
BY_LANES = (4, 1, 0, 0)
VMEM_BYTES = 16 * 2**20

ROOT, HEAD, DLK, STORE, FIXED, FULL = 0, 16, 32, 48, 64, 68
SENT_FIXED, NEAR, FAR = 60, 63, 64

GRID, PLANE, FIELD = LAYERS * WIDE, DIRS * WIDE, DIRS * LAYERS * WIDE
E, G0, G1, G2, G3, H0, H2, SC, PP, S0, SW = (i * GRID for i in range(11))
DL = 11 * GRID
DLU, DLD = DL + PLANE, DL + 2 * PLANE
KK = DL + 3 * PLANE
D1, D2, D3 = KK + FIELD, KK + 2 * FIELD, KK + 3 * FIELD
HALF = LAYERS + DIRS * LAYERS
EARLY = KK + 4 * FIELD
RR = EARLY + 4 * HALF
STATE = RR + LAYERS * ROWS


def tile(k):
    if isinstance(k, int):
        return pl.ds(k * SUB, SUB)
    return pl.ds(pl.multiple_of(k * SUB, SUB), SUB)


def odd():
    return lax.rem(lax.axis_index("space"), 2)


def gather_pack(*refs):
    hbm, (own, far), vmem, sem = refs[:7], refs[7:9], refs[9:16], refs[16]
    loads = [pltpu.make_async_copy(a, b, sem.at[i]) for i, (a, b) in enumerate(zip(hbm, vmem))]
    for load in loads[::-1]:
        load.start()
    logk, head, stor, fixed, supp, kwei, dirs = vmem
    p = odd()
    for load in loads[4:]:
        load.wait()

    def source_row(j):
        return jnp.where(p == 1, j, 3 - j)

    t = dirs[...]
    t_high = t.astype(jnp.bfloat16)
    t_low = (t - t_high.astype(jnp.float32)).astype(jnp.bfloat16)
    left = jnp.concatenate([t_high, t_low], axis=0)
    banks = dirs.shape[0] // DIRS
    places = lax.broadcasted_iota(jnp.int32, (LANE, LANE), 0).astype(jnp.bfloat16)
    half = lax.broadcasted_iota(jnp.int32, (SUB, LANE), 0) >> 2
    one, zero = jnp.bfloat16(1), jnp.bfloat16(0)

    def block(j, pair):
        r = source_row(j)
        total = [None, None]
        for s in range(BY_LANES[j], SUPPORT):
            hot, high, weight = [], [], []
            for h in range(2):
                at = (2 * pair + h) * ROWS + r
                idx = jnp.broadcast_to(supp[s, pl.ds(at, 1), :], (SUB, LANE))
                low = (idx & (LANE - 1)).astype(jnp.float32)
                low = jnp.concatenate([low, low], axis=0).astype(jnp.bfloat16)
                low = jnp.concatenate([low] * (LANE // 16), axis=0)
                hot.append(jnp.where(places == low, one, zero))
                high.append((idx >> 7) - half)
                weight.append(jnp.broadcast_to(kwei[s, pl.ds(at, 1), :], (SUB, LANE)))
            right = jnp.concatenate(hot, axis=1)
            found = jnp.dot(left, right, preferred_element_type=jnp.float32)
            found = found[: banks * DIRS] + found[banks * DIRS :]
            for h in range(2):
                value = jnp.zeros((SUB, LANE), jnp.float32)
                for m in range(banks // 2):
                    part = found[m * SUB : (m + 1) * SUB, h * LANE : (h + 1) * LANE]
                    value = jnp.where(high[h] == 2 * m, part, value)
                value = value * weight[h]
                total[h] = value if total[h] is None else total[h] + value
        for h in range(2):
            done = (0.5 * (total[h] + pltpu.roll(total[h], 4, 0)))[:DIRS]
            at = DLK * SUB + j * SUB + 2 * pair + h
            for out in (own, far) if BY_LANES[j] == 0 else (own,):
                out[pl.ds(at, DIRS, stride=ROWS * SUB), :] = done

    def by_lanes(j):
        r = source_row(j)
        rows = pl.ds(r, SUB, stride=ROWS)
        count = BY_LANES[j]
        idx = [supp[s, rows, :] for s in range(count)]
        low = [i & (LANE - 1) for i in idx]
        high = [i >> 7 for i in idx]
        found = [[jnp.zeros((SUB, LANE), jnp.float32)] * DIRS for _ in idx]
        for k in range(banks):
            hit = [h == k for h in high]
            for d in range(DIRS):
                bank = jnp.broadcast_to(dirs[pl.ds(k * DIRS + d, 1), :], (SUB, LANE))
                for s in range(count):
                    g = jnp.take_along_axis(bank, low[s], axis=1, mode="promise_in_bounds")
                    found[s][d] = jnp.where(hit[s], g, found[s][d])
        weight = [0.5 * kwei[s, rows, :] for s in range(count)]
        totals = []
        for d in range(DIRS):
            total = found[0][d] * weight[0]
            for s in range(1, count):
                total = total + found[s][d] * weight[s]
            totals.append(total)
        return totals

    def pack():
        far[tile(NEAR), :] = jnp.zeros((SUB, LANE), jnp.float32)
        for j in range(ROWS):
            r = source_row(j)
            rows = pl.ds(r, SUB, stride=ROWS)
            for l in range(LAYERS):
                k = jnp.exp(0.5 * logk[l, rows, :])
                h = head[l, rows, :]
                for out in (own, far):
                    out[tile(ROOT + l * ROWS + j), :] = k
                    out[tile(HEAD + l * ROWS + j), :] = h
                s = stor[l, rows, :]
                own[tile(STORE + l * ROWS + j), :] = s
                if j > 0:
                    far[tile(STORE + l * 3 + j - 1), :] = s
            f = fixed[rows, :].astype(jnp.float32)
            own[tile(FIXED + j), :] = f
            if j > 0:
                far[tile(SENT_FIXED + j - 1), :] = f

    lanes = {j: by_lanes(j) for j in range(ROWS) if BY_LANES[j]}
    for j in range(ROWS):
        if BY_LANES[j] < SUPPORT:
            for pair in range(4):
                block(j, pair)
        if BY_LANES[j]:
            for d in range(DIRS):
                at = tile(DLK + d * ROWS + j)
                value = lanes[j][d]
                if BY_LANES[j] < SUPPORT:
                    value = value + own[at, :]
                for out in (own, far):
                    out[at, :] = value
    for load in loads[:4]:
        load.wait()
    pack()


def near_block(own, near):
    near[: STORE * SUB, :] = own[: STORE * SUB, :]
    for l in range(LAYERS):
        rows = pl.ds((STORE + l * ROWS) * SUB, 3 * SUB)
        near[pl.ds((STORE + l * 3) * SUB, 3 * SUB), :] = own[rows, :]
    near[SENT_FIXED * SUB :, :] = own[FIXED * SUB : (FIXED + 3) * SUB, :]


def well_source(wells_hbm, rates_hbm, out, wells, rates, sem):
    loads = [
        pltpu.make_async_copy(wells_hbm, wells, sem.at[0]),
        pltpu.make_async_copy(rates_hbm, rates, sem.at[1]),
    ]
    for load in loads:
        load.start()
    p = odd()
    for load in loads:
        load.wait()
    first = lax.axis_index("space") * ROWS
    w = wells[...]
    x = ((w >> 10) & 255) - first
    place = jnp.where(p == 1, 3 - x, x) + 3
    inside = (place >= 0) & (place < 10)
    place = jnp.where(inside, ((w >> 18) * 10 + place) * SUB + ((w >> 7) & 7), -1)
    count = w.shape[1]
    rows = out.shape[0]
    hit = lax.broadcasted_iota(jnp.int32, (rows, count), 0) == place
    left = hit.astype(jnp.float32).astype(jnp.bfloat16)
    lane = lax.broadcasted_iota(jnp.int32, (LANE, count), 0) == (w & (LANE - 1))
    rest = rates[...]
    parts = []
    for _ in range(3):
        part = rest.astype(jnp.bfloat16).astype(jnp.float32)
        rest = rest - part
        parts.append(jnp.where(lane, part, 0.0).astype(jnp.bfloat16))
    total = lax.dot_general(
        left,
        jnp.concatenate(parts, axis=0),
        (((1,), (1,)), ((), ())),
        preferred_element_type=jnp.float32,
    )
    out[...] = (total[:, :LANE] + total[:, LANE : 2 * LANE]) + total[:, 2 * LANE :]


class Sweeper:
    def __init__(self, st, src):
        self.st, self.src = st, src
        lanes = lax.broadcasted_iota(jnp.int32, (SUB, LANE), 1)
        subs = lax.broadcasted_iota(jnp.int32, (SUB, LANE), 0)
        self.lane_first, self.lane_last = lanes == 0, lanes == LANE - 1
        self.sub_first, self.sub_last = subs == 0, subs == SUB - 1

    def get(self, base, i):
        return self.st[tile(base + i), :]

    def put(self, base, i, v):
        self.st[tile(base + i), :] = v

    def up(self, v):
        edge = jnp.where(self.sub_last, 0.0, pltpu.roll(v, SUB - 1, 0))
        return pltpu.roll(jnp.where(self.lane_first, edge, v), LANE - 1, 1)

    def down(self, v):
        edge = jnp.where(self.sub_first, 0.0, pltpu.roll(v, 1, 0))
        return pltpu.roll(jnp.where(self.lane_last, edge, v), 1, 1)

    def fill(self, pack, place):
        for l in range(LAYERS):
            for j in range(ROWS):
                i = l * WIDE + place(j)
                e = pack[tile(ROOT + l * ROWS + j), :]
                h = pack[tile(HEAD + l * ROWS + j), :]
                self.put(E, i, e)
                self.put(G0, i, e * h)
                self.put(H0, i, h)
        for d in range(DIRS):
            for j in range(ROWS):
                i = d * WIDE + place(j)
                v = pack[tile(DLK + d * ROWS + j), :]
                self.put(DL, i, v)
                if 0 < place(j) < WIDE - 1:
                    self.put(DLU, i, self.up(v))
                    self.put(DLD, i, self.down(v))

    def coefficients(self, w, pack, store_at, fixed_at, missing=None):
        held = pack[tile(fixed_at), :] > 0.5
        dl = [[self.get(DL, d * WIDE + w + o) for o in (-1, 0, 1)] for d in range(DIRS)]
        dlu = [self.get(DLU, d * WIDE + w) for d in range(DIRS)]
        dld = [self.get(DLD, d * WIDE + w) for d in range(DIRS)]
        for l in range(LAYERS):
            i = l * WIDE + w
            e = self.get(E, i)
            xp, xm = self.get(E, i + 1), self.get(E, i - 1)
            yp, ym = self.up(e), self.down(e)
            tall = None
            if l < LAYERS - 1:
                tall = self.get(E, i + WIDE)
            if l > 0:
                below = self.get(E, i - WIDE)
                tall = below if tall is None else tall + below
            tall = VERTICAL * tall
            total = ((xp + xm) + (yp + ym)) + tall
            store = pack[tile(store_at(l)), :]
            if missing is not None:
                store = store + missing
            inv = 1.0 / (store + e * total)
            free = jnp.where(held, 0.0, inv)
            self.put(S0, i, total)
            self.put(PP, i, free * e)
            self.put(SC, i, jnp.where(held, 1.0, store * inv))
            self.put(SW, i, self.src[tile(l * 10 + w - 1), :] * free)
            for d in range(DIRS):
                k = xp * dl[d][2] + xm * dl[d][0] + yp * dlu[d] + ym * dld[d] + tall * dl[d][1]
                self.put(KK, (d * LAYERS + l) * WIDE + w, k)

    def base_sides(self, number, w):
        prev = (G0, G1, G2, G3)[number - 1]
        here = [self.get(prev, l * WIDE + w) for l in range(LAYERS)]
        return [
            (self.get(prev, l * WIDE + w + 1), self.up(g), self.down(g), self.tall(here, l))
            for l, g in enumerate(here)
        ]

    def tall(self, here, l):
        beside = [here[k] for k in (l - 1, l + 1) if 0 <= k < LAYERS]
        return VERTICAL * (beside[0] if len(beside) == 1 else beside[0] + beside[1])

    def tangent_sides(self, number, w, d, sides):
        dprev = (None, D1, D2, D3)[number - 1]
        p = d * WIDE + w
        here, after = self.get(DL, p), self.get(DL, p + 1)
        plus, minus = self.get(DLU, p), self.get(DLD, p)
        sums = [(xp * after + tall * here) + (yp * plus + ym * minus) for xp, yp, ym, tall in sides]
        if dprev is not None:
            at = [(d * LAYERS + l) * WIDE + w for l in range(LAYERS)]
            v = [self.get(dprev, f) for f in at]
            sums = [
                acc + ((self.up(v[l]) + self.down(v[l])) + (self.get(dprev, at[l] + 1) + self.tall(v, l)))
                for l, acc in enumerate(sums)
            ]
        return sums

    def early(self, number, w):
        at = (number - 1) * HALF
        sides = self.base_sides(number, w)
        for l, (xp, yp, ym, tall) in enumerate(sides):
            self.put(EARLY, at + l, (xp + tall) + (yp + ym))
        for d in range(DIRS):
            for l, acc in enumerate(self.tangent_sides(number, w, d, sides)):
                self.put(EARLY, at + LAYERS + d * LAYERS + l, acc)

    def base_row(self, number, w, late=False, out=None):
        start = H0 if number < 3 else H2
        prev = (G0, G1, G2, G3)[number - 1]
        new = (G1, G2, G3, None)[number - 1]
        get = self.get
        at = (number - 1) * HALF
        sides = None if late else self.base_sides(number, w)
        base = []
        for l in range(LAYERS):
            i = l * WIDE + w
            if late:
                total = get(EARLY, at + l)
            else:
                xp, yp, ym, tall = sides[l]
                total = (xp + tall) + (yp + ym)
            xm = get(prev, i - 1)
            total = total + xm
            e, sc, pp = get(E, i), get(SC, i), get(PP, i)
            value = sc * get(start, i) + get(SW, i) + pp * total
            if new is not None:
                self.put(new, i, e * value)
            if number == 2:
                self.put(H2, i, value)
            if out is not None:
                out[0][l, out[1], :] = value
            scaled, kept = pp * e, sc
            if out is not None:
                scaled, kept = pp, sc * get(RR, l * ROWS + w - 4)
            base.append((xm, value, total - value * get(S0, i), scaled, kept))
        return sides, base

    def tangent_row(self, number, w, d, sides, base, out=None):
        dprev = (None, D1, D2, D3)[number - 1]
        dnew = (D1, D2, D3, None)[number - 1]
        get = self.get
        if sides is None:
            at = (number - 1) * HALF + LAYERS + d * LAYERS
            sums = [get(EARLY, at + l) for l in range(LAYERS)]
        else:
            sums = self.tangent_sides(number, w, d, sides)
        p = d * WIDE + w
        here, before = get(DL, p), get(DL, p - 1)
        for l, (xm, value, own, scaled, kept) in enumerate(base):
            f = (d * LAYERS + l) * WIDE + w
            acc = sums[l] + xm * before
            if dprev is not None:
                acc = acc + get(dprev, f - 1)
            acc = acc + (own * here - value * get(KK, f))
            result = scaled * acc
            if number > 2:
                result = result + kept * get(D2, f)
            if out is None:
                self.put(dnew, f, result)
            else:
                out[0][d, l, out[1], :] = result

    def sweep(self, number, w, late=False):
        sides, base = self.base_row(number, w, late)
        for d in range(DIRS):
            self.tangent_row(number, w, d, sides, base)

    def rows(self, number, lo, hi):
        for w in range(lo, hi):
            self.sweep(number, w)


def before_far(own, near, src, st):
    s = Sweeper(st, src)
    s.fill(own, lambda j: 7 - j)
    s.fill(near, lambda j: 8 + j)

    for w in range(5, 8):
        s.coefficients(w, own, lambda l: STORE + l * ROWS + 7 - w, FIXED + 7 - w)
    for w in range(8, 11):
        s.coefficients(w, near, lambda l: STORE + l * 3 + w - 8, SENT_FIXED + w - 8)
    s.rows(1, 5, 11)
    s.rows(2, 6, 10)
    s.rows(3, 7, 9)
    for i in range(LAYERS * ROWS):
        l, w = divmod(i, ROWS)
        s.put(RR, i, 1.0 / s.get(E, l * WIDE + w + 4))
    for number in range(1, 5):
        s.early(number, number + 3)


def after_far(own, far, src, st_in, head_out, sens_out, st, head, sens, sem):
    del st_in
    me = lax.axis_index("space")
    inside = (me > 0) & (me < lax.axis_size("space") - 1)
    missing = jnp.where(inside, 0.0, 1.0).astype(jnp.float32)
    s = Sweeper(st, src)
    s.fill(far, lambda j: j)

    for w in range(1, 4):
        s.coefficients(
            w, far, lambda l: STORE + l * 3 + w - 1, SENT_FIXED + w - 1, missing
        )
    s.coefficients(4, own, lambda l: STORE + l * ROWS + 3, FIXED + 3)
    for number in range(1, 4):
        for w in range(number + 3, number - 1, -1):
            s.sweep(number, w, late=w == number + 3)
    p = odd()
    rows = {w: pl.ds(jnp.where(p == 1, 7 - w, w - 4), SUB, stride=ROWS) for w in range(4, 8)}
    base = {w: s.base_row(4, w, w == 7, (head, rows[w])) for w in rows}
    stores = [pltpu.make_async_copy(head, head_out, sem.at[DIRS])]
    stores[0].start()
    for d in range(DIRS):
        for w in (5, 6, 7, 4):
            s.tangent_row(4, w, d, *base[w], (sens, rows[w]))
        stores.append(pltpu.make_async_copy(sens.at[d], sens_out.at[d], sem.at[d]))
        stores[-1].start()
    for store in stores:
        store.wait()


def tiles(x):
    lead, rows, width = x.shape
    x = x.reshape(lead, rows, width // LANE, LANE).transpose(0, 2, 1, 3)
    return x.reshape(lead, rows * width // LANE, LANE)


def rows_back(x, lead):
    x = x.reshape(*lead, SUB, ROWS, LANE)
    x = jnp.swapaxes(x, -3, -2)
    return x.reshape(*lead, ROWS, SUB * LANE)


def local(logk, storage, head0, support, kweight, fixed, directions, wells, rates):
    f32 = jnp.float32
    vmem = pl.BlockSpec(memory_space=pltpu.VMEM)
    hbm = pl.BlockSpec(memory_space=pltpu.HBM)
    logk, storage, head0, support, kweight = map(
        tiles, (logk, storage, head0, support, kweight)
    )
    fixed = tiles(fixed[None])[0]
    table = tiles(directions[None])[0]
    inputs = [
        pltpu.with_memory_space_constraint(x, pltpu.HBM)
        for x in (logk, head0, storage, fixed, support, kweight, table)
    ]
    count = lax.axis_size("space")
    own, far = pl.pallas_call(
        gather_pack,
        out_shape=(
            pltpu.VMEM((FULL * SUB, LANE), f32),
            pltpu.VMEM((FAR * SUB, LANE), f32),
        ),
        in_specs=[hbm] * 7,
        out_specs=(vmem,) * 2,
        scratch_shapes=[pltpu.VMEM(x.shape, x.dtype) for x in inputs]
        + [pltpu.SemaphoreType.DMA((7,))],
        compiler_params=pltpu.CompilerParams(vmem_limit_bytes=VMEM_BYTES),
        name="gather_pack",
    )(*inputs)
    far = lax.ppermute(
        far,
        "space",
        [(i, i + 1 if i % 2 else i - 1) for i in range(1, count - 1)],
    )
    near = pl.pallas_call(
        near_block,
        out_shape=pltpu.VMEM((NEAR * SUB, LANE), f32),
        in_specs=[vmem],
        out_specs=vmem,
        compiler_params=pltpu.CompilerParams(vmem_limit_bytes=VMEM_BYTES),
        name="near_block",
    )(own)
    near = lax.ppermute(near, "space", [(i, i ^ 1) for i in range(count)])
    src = pl.pallas_call(
        well_source,
        out_shape=pltpu.VMEM((LAYERS * 10 * SUB, LANE), f32),
        in_specs=[hbm] * 2,
        out_specs=vmem,
        scratch_shapes=[
            pltpu.VMEM((1, wells.shape[0]), wells.dtype),
            pltpu.VMEM((1, rates.shape[0]), rates.dtype),
            pltpu.SemaphoreType.DMA((2,)),
        ],
        compiler_params=pltpu.CompilerParams(vmem_limit_bytes=VMEM_BYTES),
        name="well_source",
    )(*(pltpu.with_memory_space_constraint(x[None], pltpu.HBM) for x in (wells, rates)))
    state = pl.pallas_call(
        before_far,
        out_shape=pltpu.VMEM((STATE * SUB, LANE), f32),
        in_specs=[vmem] * 3,
        out_specs=vmem,
        compiler_params=pltpu.CompilerParams(vmem_limit_bytes=VMEM_BYTES),
        cost_estimate=pl.CostEstimate(flops=0, bytes_accessed=0, transcendentals=0),
        name="before_far",
    )(own, near, src)
    head, sens, _ = pl.pallas_call(
        after_far,
        out_shape=(
            pltpu.HBM((LAYERS, SUB * ROWS, LANE), f32),
            pltpu.HBM((DIRS, LAYERS, SUB * ROWS, LANE), f32),
            pltpu.VMEM((STATE * SUB, LANE), f32),
        ),
        in_specs=[vmem] * 4,
        out_specs=(hbm, hbm, vmem),
        scratch_shapes=[
            pltpu.VMEM((LAYERS, SUB * ROWS, LANE), f32),
            pltpu.VMEM((DIRS, LAYERS, SUB * ROWS, LANE), f32),
            pltpu.SemaphoreType.DMA((DIRS + 1,)),
        ],
        input_output_aliases={3: 2},
        compiler_params=pltpu.CompilerParams(vmem_limit_bytes=VMEM_BYTES),
        name="after_far",
    )(own, far, src, state)
    return rows_back(head, (LAYERS,)), rows_back(sens, (DIRS, LAYERS))


def solution(mesh):
    rows = P(None, "space", None)
    return jax.shard_map(
        local,
        mesh=mesh,
        in_specs=(rows,) * 5 + (P("space", None), P("dir", None), P(), P()),
        out_specs=(rows, P("dir", None, "space", None)),
        check_vma=False,
    )
```
